256 devices in a mesh: inst: 32 (over x, z), tp: 8 (over y, core).
Axes of the slice: x: 4, y: 4, z: 8, core: 2. Of those that a mesh axis runs over, the one named last changes fastest.
Arguments:
- ssm_state: bfloat16 [256, 256, 64, 256], P('inst', 'tp'), may hold values from -6 to 6
- conv_tail: bfloat16 [256, 3, 20480], P('inst', None, 'tp'), may hold values from -6 to 6
- kv_pool: bfloat16 [1024, 2, 128, 1024], P('inst', None, 'tp'), may hold values from -6 to 6
- page_table: int32 [256, 4], P('inst'), may hold values from 0 to 31, as said below
- lengths: int32 [256], replicated, may hold values from 1 to 512
- move_src: int32 [32], replicated, may hold values from 0 to 255, as said below
- move_dst: int32 [32], replicated, may hold values from 0 to 255, as said below
- x_in: bfloat16 [256, 2, 20480], P('inst', None, 'tp'), may hold values from -6 to 6
- z_gate: bfloat16 [256, 2, 16384], P('inst', None, 'tp'), may hold values from -6 to 6
- dt_raw: float32 [256, 2, 256], P('inst', None, 'tp'), may hold values from -6 to 6
- queries: bfloat16 [256, 2, 8192], P('inst', None, 'tp'), may hold values from -64 to 64
- new_kv: bfloat16 [256, 2, 2, 1024], P('inst', None, None, 'tp'), may hold values from -6 to 6
- a_log: float32 [256], P('tp'), may hold values from -1 to 2.5
- dt_bias: float32 [256], P('tp'), may hold values from -4 to 0.5
- skip_d: float32 [256], P('tp'), may hold values from 0.5 to 2
- conv_w: float32 [4, 20480], P(None, 'tp'), may hold values from -3 to 3
- norm_gain: float32 [16384], P('tp'), may hold values from 0.1 to 1.9
Outputs:
- mamba_out: bfloat16 [256, 2, 16384], P('inst', None, 'tp')
- attn_out: bfloat16 [256, 2, 8192], P('inst', None, 'tp')
- arrived_state: bfloat16 [32, 256, 64, 256], P('inst', 'tp')
- arrived_pages: bfloat16 [128, 2, 128, 1024], P('inst', None, 'tp')
The draws below stay inside these ranges and needn't reach their ends.
Inputs may be any that keep to these rules, and one draw needn't show every extreme that they name: `move_src`: entries k * 1 to (k + 1) - 1 are distinct slots of instance k, that is of k * 8 to (k + 1) * 8 - 1. move_dst holds the same slots as move_src in another order, so every instance receives exactly 1 request. `page_table`: the rows of one instance name each of its 32 pages exactly once.
All inputs are finite; a program needn't handle non-finite values.
Results may differ from the reference program's by a relative error of at most 0.002.
Values may be sent and summed in bfloat16 or wider, within the bound.
No kernel may reach another device: no remote copies, remote signals or barrier semaphores. Data moves between devices by JAX's collectives and lax.ppermute only.
A program may use at most 128 MiB of HBM per device.

```python
import jax
import jax.numpy as jnp
from jax import lax

HEADS = 256
HEAD_P = 64
STATE_N = 256
CONV_K = 4
KVH = 8
HEAD_D = 128
PAGE = 128
PPR = 4
REQ_DEV = 8
MOVE = 1
INNER = 16384
CONV_CH = 20480
QD = 8192
KVD = 1024
SLOTS = 256
MOVES = 32
POOL_DEV = 32
POOL = 1024
N_INST = 32


def migration_lists(key):
    pick_keys = jax.random.split(key, N_INST)
    chosen = jax.vmap(lambda subkey: jax.random.permutation(subkey, REQ_DEV)[:MOVE])(pick_keys)
    leaving = (chosen + (jnp.arange(N_INST) * REQ_DEV)[:, None]).reshape(-1).astype(jnp.int32)
    cycle_order = jax.random.permutation(jax.random.fold_in(key, 11), MOVES)
    arriving = jnp.zeros((MOVES,), jnp.int32).at[cycle_order].set(leaving[jnp.roll(cycle_order, -1)])
    return (leaving, arriving)


def draw_move_src(key, part):
    leaving, arriving = migration_lists(key)
    return leaving


def draw_move_dst(key, part):
    leaving, arriving = migration_lists(key)
    return arriving


def draw_page_table(key, part):
    key = jax.random.fold_in(key, 3)
    pool_keys = jax.random.split(key, N_INST)
    shuffled = jax.vmap(lambda subkey: jax.random.permutation(subkey, POOL_DEV))(pool_keys)
    return shuffled.reshape(SLOTS, PPR).astype(jnp.int32)


def draw_queries(key, part):
    key = jax.random.fold_in(key, 5)
    return jnp.clip(jax.random.normal(key, (SLOTS, 2, QD)), -6.0, 6.0).astype(jnp.bfloat16)


def with_ends(result, key, least, largest):
    index_at = [jax.random.randint(jax.random.fold_in(key, axis), (), 0, length) for axis, length in enumerate(result.shape)]
    longest = result.shape.index(max(result.shape))
    beside = index_at[:longest] + [(index_at[longest] + 1) % result.shape[longest]] + index_at[longest + 1:]
    return result.at[tuple(index_at)].set(least).at[tuple(beside)].set(largest)


def levels(stream_key, dims, shards, low, top_value):
    factor_of, own = 1.0, jax.random.fold_in(stream_key, 6)
    for axis_at, parts in shards:
        steps = jnp.exp(jax.random.uniform(jax.random.fold_in(own, axis_at), (parts,), jnp.float32, low / len(shards), top_value / len(shards)))
        factor_of = factor_of * jnp.repeat(steps, dims[axis_at] // parts).reshape([-1 if axis == axis_at else 1 for axis in range(len(dims))])
    return factor_of


def bell_draw(own_key, dims, deviation, reach, pieces=(), held_as=jnp.bfloat16):
    drawn = deviation * jax.random.normal(own_key, dims, jnp.float32)
    if pieces:
        drawn = drawn * levels(own_key, dims, pieces, -0.22, 0.18)
    return jnp.clip(drawn, -reach, reach).astype(held_as)


def setup_inputs(seed: int = 0) -> dict:
    streams_of = jax.random.split(jax.random.key(seed), 18)
    return {
        "ssm_state": bell_draw(streams_of[0], (SLOTS, HEADS, HEAD_P, STATE_N), 1.0, 6.0, ((0, 32), (1, 8))),
        "conv_tail": bell_draw(streams_of[1], (SLOTS, CONV_K - 1, CONV_CH), 1.0, 6.0, ((0, 32), (2, 8))),
        "kv_pool": bell_draw(streams_of[2], (POOL, 2, PAGE, KVD), 1.0, 6.0, ((0, 32), (2, 8))),
        "page_table": draw_page_table(jax.random.fold_in(streams_of[17], 71), 0),
        "lengths": with_ends(jax.random.randint(streams_of[4], (SLOTS,), 1, PPR * PAGE + 1), jax.random.fold_in(streams_of[4], 1), 1, PPR * PAGE).astype(jnp.int32),
        "move_src": draw_move_src(jax.random.fold_in(streams_of[17], 71), 0),
        "move_dst": draw_move_dst(jax.random.fold_in(streams_of[17], 71), 0),
        "x_in": bell_draw(streams_of[7], (SLOTS, 2, CONV_CH), 1.0, 6.0, ((0, 32), (2, 8))),
        "z_gate": bell_draw(streams_of[8], (SLOTS, 2, INNER), 1.0, 6.0, ((0, 32), (2, 8))),
        "dt_raw": bell_draw(streams_of[9], (SLOTS, 2, HEADS), 1.0, 6.0, ((0, 32), (2, 8)), jnp.float32),
        "queries": draw_queries(jax.random.fold_in(streams_of[17], 71), 0),
        "new_kv": bell_draw(streams_of[11], (SLOTS, 2, 2, KVD), 1.0, 6.0, ((0, 32), (3, 8))),
        "a_log": jnp.clip(-1.0 + 3.5 * jax.random.uniform(streams_of[12], (HEADS,), jnp.float32) ** levels(streams_of[12], (HEADS,), ((0, 8),), -0.2, 0.2), -1.0, 2.5),
        "dt_bias": jnp.clip(-4.0 + 4.5 * jax.random.uniform(streams_of[13], (HEADS,), jnp.float32) ** levels(streams_of[13], (HEADS,), ((0, 8),), -0.2, 0.2), -4.0, 0.5),
        "skip_d": jnp.clip(0.5 + 1.5 * jax.random.uniform(streams_of[14], (HEADS,), jnp.float32) ** levels(streams_of[14], (HEADS,), ((0, 8),), -0.2, 0.2), 0.5, 2.0),
        "conv_w": bell_draw(streams_of[15], (CONV_K, CONV_CH), CONV_K ** -0.5, 3.0, ((1, 8),), jnp.float32),
        "norm_gain": jnp.clip(1.0 + 0.18 * jax.random.normal(streams_of[16], (INNER,), jnp.float32), 0.1, 1.9),
    }


def mamba_steps(state, tail, fresh, gate_z, dt_in, a_log, dt_bias, skip_d, conv_w, gain):
    head_count, width_p, width_n = state.shape
    g_here = (tail.shape[-1] - head_count * width_p) // (2 * width_n)
    per_group = head_count // g_here
    x_width = per_group * width_p
    carried = state.astype(jnp.float32)
    window = jnp.concatenate([tail.astype(jnp.float32), fresh.astype(jnp.float32)], 0)
    tap_count = conv_w.shape[0]
    decay_rate = jnp.exp(a_log)
    results = []
    for step_index in range(2):
        convolved = jax.nn.silu(lax.optimization_barrier(jnp.sum(conv_w * window[step_index:step_index + tap_count], 0)))
        grouped = convolved.reshape(g_here, x_width + 2 * width_n)
        values = grouped[:, :x_width].reshape(head_count, width_p)
        b_in = jnp.repeat(grouped[:, x_width:x_width + width_n], per_group, axis=0)
        c_out = jnp.repeat(grouped[:, x_width + width_n:], per_group, axis=0)
        step_size = jax.nn.softplus(dt_in[step_index] + dt_bias)
        retain = jnp.exp(-step_size * decay_rate)
        carried = carried * retain[:, None, None] + (step_size[:, None] * values)[:, :, None] * b_in[:, None, :]
        output_rows = lax.optimization_barrier(jnp.sum(carried * c_out[:, None, :], -1)) + skip_d[:, None] * values
        gate_rows = jax.nn.silu(gate_z[step_index].astype(jnp.float32)).reshape(g_here, x_width)
        output_rows = output_rows.reshape(g_here, x_width) * gate_rows
        output_rows = output_rows * lax.rsqrt(lax.optimization_barrier(jnp.mean(output_rows * output_rows, -1, keepdims=True)) + 1e-05)
        results.append((output_rows.reshape(-1) * gain).astype(jnp.bfloat16))
    return (jnp.stack(results), carried.astype(jnp.bfloat16))

def partial_scores(query_pair, key_rows, value_rows, valid, fresh, fresh_on):
    kv_heads = key_rows.shape[1]
    head_dim = key_rows.shape[2]
    q_heads = query_pair.shape[-1] // head_dim
    group_size = q_heads // kv_heads
    scaled = query_pair.astype(jnp.float32).reshape(2, kv_heads, group_size, head_dim) * head_dim ** (-0.5)
    fresh_keys = fresh[:, 0].astype(jnp.float32).reshape(2, kv_heads, head_dim)
    fresh_values = fresh[:, 1].astype(jnp.float32).reshape(2, kv_heads, head_dim)
    all_keys = jnp.concatenate([key_rows.astype(jnp.float32), fresh_keys], 0)
    all_values = jnp.concatenate([value_rows.astype(jnp.float32), fresh_values], 0)
    scores = jnp.einsum('tgsd,lgd->tgsl', scaled, all_keys, precision=lax.Precision.HIGHEST)
    step_rows = jnp.arange(2, dtype=jnp.int32)
    fresh_mask = (step_rows[None, :] <= step_rows[:, None]) & fresh_on
    allowed = jnp.concatenate([jnp.broadcast_to(valid[None, :], (2, valid.shape[0])), fresh_mask], 1)
    allowed = allowed[:, None, None, :]
    peak_score = lax.optimization_barrier(jnp.max(jnp.where(allowed, scores, -1e+30), -1))
    weights = jnp.where(allowed, jnp.exp(scores - peak_score[..., None]), 0.0)
    weight_sum = lax.optimization_barrier(jnp.sum(weights, -1))
    weighted = jnp.einsum('tgsl,lgd->tgsd', weights, all_values, precision=lax.Precision.HIGHEST)
    return (peak_score.reshape(2, q_heads), weight_sum.reshape(2, q_heads), weighted.reshape(2, q_heads, head_dim))

def reference(ssm_state, conv_tail, kv_pool, page_table, lengths, move_src, move_dst, x_in, z_gate, dt_raw, queries, new_kv, a_log, dt_bias, skip_d, conv_w, norm_gain):
    slot_ids = jnp.arange(SLOTS, dtype=jnp.int32)
    anchor = slot_ids.at[move_dst].set(move_src)
    global_pages = (slot_ids // REQ_DEV)[:, None] * POOL_DEV + page_table
    positions = jnp.arange(PPR * PAGE, dtype=jnp.int32)

    def one_slot(slot_index):
        anchor_slot = anchor[slot_index]
        mixed, unused = mamba_steps(ssm_state[anchor_slot], conv_tail[anchor_slot], x_in[slot_index], z_gate[slot_index], dt_raw[slot_index], a_log, dt_bias, skip_d, conv_w, norm_gain)
        fetched = kv_pool[global_pages[anchor_slot]]
        key_rows = fetched[:, 0].reshape(PPR * PAGE, KVH, HEAD_D)
        value_rows = fetched[:, 1].reshape(PPR * PAGE, KVH, HEAD_D)
        valid = positions < lengths[anchor_slot]
        peak_score, weight_sum, weighted = partial_scores(queries[slot_index], key_rows, value_rows, valid, new_kv[slot_index], True)
        attended = (weighted / weight_sum[..., None]).reshape(2, QD).astype(jnp.bfloat16)
        return (mixed, attended)
    mamba_out, attn_out = lax.map(one_slot, slot_ids)
    by_arrival = jnp.argsort(move_dst, stable=True)
    land_slots = move_dst[by_arrival]
    from_slots = move_src[by_arrival]

    def one_arrival(pair_rows):
        landing, anchor_slot = pair_rows
        unused, final_state = mamba_steps(ssm_state[anchor_slot], conv_tail[anchor_slot], x_in[landing], z_gate[landing], dt_raw[landing], a_log, dt_bias, skip_d, conv_w, norm_gain)
        return final_state
    arrived_state = lax.map(one_arrival, (land_slots, from_slots))
    arrived_pages = kv_pool[global_pages[from_slots]].reshape(MOVES * PPR, 2, PAGE, KVD)
    return (mamba_out, attn_out, arrived_state, arrived_pages)
```

```python
import functools

import jax
import jax.numpy as jnp
from jax import lax
from jax.experimental import pallas as pl
from jax.experimental.pallas import tpu as pltpu
from jax.sharding import PartitionSpec as P

BF = jnp.bfloat16
F32 = jnp.float32
HEADS = 32
HEAD_P = 64
INNER = 2048
STATE_N = 256
CONV = 2560
HEAD_D = 128
PAGE = 128
PPR = 4
TP = 8
TOK = 16
N_INST = 32
SLOTS = 8
PAGE_AT = 128
TAIL_AT = 160
ROWS = 168
TAIL_ROWS = 60

SMEM = pl.BlockSpec(memory_space=pltpu.SMEM)
VMEM = pl.BlockSpec(memory_space=pltpu.VMEM)
ANY = pl.BlockSpec(memory_space=pl.ANY)


def params(mib=48):
    return pltpu.CompilerParams(vmem_limit_bytes=mib * 1024 * 1024)


def cost(microseconds):
    return pl.CostEstimate(
        flops=int(microseconds * 5e8), bytes_accessed=int(microseconds * 3e6), transcendentals=0
    )


def halves(value):
    high = value.astype(BF)
    low = (value - high.astype(F32)).astype(BF)
    return high, low


def thirds(value):
    high = value.astype(BF)
    rest = value - high.astype(F32)
    middle = rest.astype(BF)
    low = (rest - middle.astype(F32)).astype(BF)
    return high, middle, low


def dot_nt(left, right):
    return lax.dot_general(left, right, (((1,), (1,)), ((), ())), preferred_element_type=F32)


def dot_nn(left, right):
    return lax.dot_general(left, right, (((1,), (0,)), ((), ())), preferred_element_type=F32)


def pack_kernel(idx, move_src, table, state, tail, pool, out, pages, tail_rows, state_sems, page_sems):
    leave = move_src[idx[0]] & (SLOTS - 1)
    copies = []
    for half in range(2):
        copies.append(
            pltpu.make_async_copy(
                state.at[leave, :, :, pl.ds(half * 128, 128)],
                out.at[:, pl.ds(half * 64, 64), :],
                state_sems.at[half],
            )
        )
    for page in range(PPR):
        copies.append(
            pltpu.make_async_copy(pool.at[table[page, leave]], pages.at[page], page_sems.at[page])
        )
    for copy in copies:
        copy.start()
    slot = lax.broadcasted_iota(jnp.int32, (3, SLOTS, CONV), 1)
    mine = jnp.sum(jnp.where(slot == leave, tail[...].astype(F32), 0.0), 1)
    tail_rows[...] = jnp.zeros_like(tail_rows)
    for row in range(TAIL_ROWS):
        tap, at = row // 20, (row % 20) * 128
        tail_rows[row // 2, row % 2 : row % 2 + 1, :] = mine[tap : tap + 1, at : at + 128]
    out[:, TAIL_AT:ROWS, :] = tail_rows[...].astype(BF)
    for copy in copies[2:]:
        copy.wait()
    for kv in range(2 * PPR):
        for head in range(TP):
            at = PAGE_AT + TOK * (head % 2)
            out[kv * 4 + head // 2, at : at + TOK, :] = pages[
                kv // 2, kv % 2, :, head * 128 : head * 128 + 128
            ]
    for copy in copies[:2]:
        copy.wait()


def pack(idx, move_src, table, state, tail, pool):
    return pl.pallas_call(
        pack_kernel,
        out_shape=jax.ShapeDtypeStruct((N_INST, ROWS, 128), BF),
        in_specs=[SMEM, SMEM, SMEM, ANY, VMEM, ANY],
        out_specs=VMEM,
        scratch_shapes=[
            pltpu.VMEM((PPR, 2, TOK, TP * 128), BF),
            pltpu.VMEM((N_INST, 8, 128), F32),
            pltpu.SemaphoreType.DMA((2,)),
            pltpu.SemaphoreType.DMA((PPR,)),
        ],
        compiler_params=params(),
        cost_estimate=cost(3),
    )(idx, move_src, table, state, tail, pool)


def reorder_kernel(move_dst, shares, out, sems):
    copies = [
        pltpu.make_async_copy(shares.at[j], out.at[move_dst[j] >> 3], sems.at[j])
        for j in range(N_INST)
    ]
    for copy in copies:
        copy.start()
    for copy in copies:
        copy.wait()


def reorder(move_dst, shares):
    return pl.pallas_call(
        reorder_kernel,
        out_shape=jax.ShapeDtypeStruct(shares.shape, shares.dtype),
        in_specs=[SMEM, ANY],
        out_specs=ANY,
        scratch_shapes=[pltpu.SemaphoreType.DMA((N_INST,))],
        compiler_params=params(),
        cost_estimate=cost(3),
    )(move_dst, shares)


def unpack_kernel(shares, arrived, send):
    for kv in range(2 * PPR):
        for head in range(TP):
            at = TOK * (head % 2)
            block = shares[kv * 4 + head // 2, at : at + TOK, :]
            arrived[kv // 2, kv % 2, :, head * 128 : head * 128 + 128] = block
            send[head, kv] = block


def unpack(shares):
    return pl.pallas_call(
        unpack_kernel,
        grid=(1,),
        out_shape=(
            jax.ShapeDtypeStruct((PPR, 2, TOK, TP * 128), BF),
            jax.ShapeDtypeStruct((TP, 2 * PPR, TOK, 128), BF),
        ),
        in_specs=[pl.BlockSpec((N_INST, 32, 128), lambda i: (0, PAGE_AT // 32, 0))],
        out_specs=(
            pl.BlockSpec((PPR, 2, TOK, TP * 128), lambda i: (0, 0, 0, 0)),
            pl.BlockSpec((TP, 2 * PPR, TOK, 128), lambda i: (0, 0, 0, 0)),
        ),
        compiler_params=params(),
        cost_estimate=cost(1),
    )(shares)


def split_heads_kernel(idx, pool, *refs):
    outs, sems = refs[:TP], refs[TP]
    copies = []
    for d in range(TP):
        at = pl.multiple_of((idx[1] ^ d) * 128, 128)
        copies.append(pltpu.make_async_copy(pool.at[:, :, :, pl.ds(at, 128)], outs[d], sems.at[d]))
    for copy in copies:
        copy.start()
    for copy in copies:
        copy.wait()


def split_heads(idx, pool):
    piece = jax.ShapeDtypeStruct(pool.shape[:3] + (128,), BF)
    return pl.pallas_call(
        split_heads_kernel,
        out_shape=(piece,) * TP,
        in_specs=[SMEM, ANY],
        out_specs=(ANY,) * TP,
        scratch_shapes=[pltpu.SemaphoreType.DMA((TP,))],
        compiler_params=params(),
        cost_estimate=cost(3),
    )(idx, pool)


def silu(value):
    return value * (1.0 / (1.0 + jnp.exp(-value)))


def mixer(state_dots, tail, fresh, gate, dt_raw, a_log, dt_bias, skip, conv_w, gain):
    window = [tail[k : k + 1] for k in range(3)] + [fresh[k : k + 1] for k in range(2)]
    steps = []
    for t in range(2):
        total = conv_w[0:1] * window[t]
        for k in range(1, 4):
            total = total + conv_w[k : k + 1] * window[t + k]
        steps.append(total)
    conv = silu(jnp.concatenate(steps, 0))
    x = conv[:, :INNER]
    b_in = conv[:, INNER : INNER + STATE_N]
    c_out = conv[:, INNER + STATE_N :]

    raw = dt_raw + dt_bias
    step = jnp.maximum(raw, 0.0) + jnp.log1p(jnp.exp(-jnp.abs(raw)))
    retain = jnp.exp(-step * jnp.exp(a_log))
    per_head = jnp.concatenate([step, retain, skip, jnp.zeros((3, HEADS), F32)], 0)
    head_row = lax.broadcasted_iota(jnp.int32, (HEADS, INNER), 0)
    channel = lax.broadcasted_iota(jnp.int32, (HEADS, INNER), 1)
    spread = jnp.where(channel // HEAD_P == head_row, 1.0, 0.0).astype(BF)
    spread_out = sum(dot_nn(part, spread) for part in thirds(per_head))
    step1, step2 = spread_out[0:1], spread_out[1:2]
    keep1, keep2 = spread_out[2:3], spread_out[3:4]
    skip_c = spread_out[4:5]

    c_high, c_low = halves(c_out)
    dots = state_dots(jnp.concatenate([c_high, c_low, jnp.zeros((12, STATE_N), BF)], 0))
    dots = dots[0:2] + dots[2:4]
    b1, b2, c1, c2 = b_in[0:1], b_in[1:2], c_out[0:1], c_out[1:2]
    x1, x2 = x[0:1], x[1:2]
    u1, u2 = step1 * x1, step2 * x2
    bc11 = jnp.sum(b1 * c1, -1, keepdims=True)
    bc12 = jnp.sum(b1 * c2, -1, keepdims=True)
    bc22 = jnp.sum(b2 * c2, -1, keepdims=True)
    y1 = keep1 * dots[0:1] + u1 * bc11 + skip_c * x1
    y2 = keep2 * (keep1 * dots[1:2] + u1 * bc12) + u2 * bc22 + skip_c * x2
    y = jnp.concatenate([y1, y2], 0) * silu(gate)
    y = y * lax.rsqrt(jnp.mean(y * y, -1, keepdims=True) + 1e-05) * gain
    return y.astype(BF), (keep2 * u1, u2, b1, b2, keep1 * keep2)


def mixer_all_kernel(state, tail, fresh, gate, dt_raw, a_log, dt_bias, skip, conv_w, gain, out):
    here = pl.program_id(0)
    slot = lax.broadcasted_iota(jnp.int32, (3, SLOTS, CONV), 1)
    mine = jnp.sum(jnp.where(slot == here, tail[...].astype(F32), 0.0), 1)
    rows = state[0].reshape(INNER, STATE_N)
    y, _ = mixer(
        lambda lhs: dot_nt(lhs, rows),
        mine,
        fresh[0].astype(F32),
        gate[0].astype(F32),
        dt_raw[0],
        a_log[...],
        dt_bias[...],
        skip[...],
        conv_w[...],
        gain[...],
    )
    out[0] = y


def mixer_all(state, tail, fresh, gate, dt_raw, a_log, dt_bias, skip, conv_w, gain):
    def whole(shape):
        return pl.BlockSpec(shape, lambda s: (0,) * len(shape))

    def by_slot(shape):
        return pl.BlockSpec((1,) + shape, lambda s: (s,) + (0,) * len(shape))

    return pl.pallas_call(
        mixer_all_kernel,
        grid=(SLOTS,),
        out_shape=jax.ShapeDtypeStruct((SLOTS, 2, INNER), BF),
        in_specs=[
            by_slot((HEADS, HEAD_P, STATE_N)),
            whole((3, SLOTS, CONV)),
            by_slot((2, CONV)),
            by_slot((2, INNER)),
            by_slot((2, HEADS)),
            whole((1, HEADS)),
            whole((1, HEADS)),
            whole((1, HEADS)),
            whole((4, CONV)),
            whole((1, INNER)),
        ],
        out_specs=by_slot((2, INNER)),
        compiler_params=params(),
        cost_estimate=cost(16),
    )(state, tail, fresh, gate, dt_raw, a_log, dt_bias, skip, conv_w, gain)


def mixer_landed_kernel(
    idx, move_src, shares, fresh, gate, dt_raw, a_log, dt_bias, skip, conv_w, gain, others, out, final
):
    land = move_src[idx[0]] & (SLOTS - 1)
    pieces = shares[:, TAIL_AT:ROWS, :].astype(F32)
    tail = jnp.concatenate(
        [
            jnp.concatenate(
                [pieces[row // 2, row % 2 : row % 2 + 1, :] for row in range(tap * 20, tap * 20 + 20)], 1
            )
            for tap in range(3)
        ],
        0,
    )
    left = shares[:, 0:64, :].reshape(INNER, 128)
    right = shares[:, 64:128, :].reshape(INNER, 128)
    y, (a1, a2, b1, b2, keep) = mixer(
        lambda lhs: dot_nt(lhs[:, :128], left) + dot_nt(lhs[:, 128:], right),
        tail,
        fresh[land].astype(F32),
        gate[land].astype(F32),
        dt_raw[land],
        a_log[...],
        dt_bias[...],
        skip[...],
        conv_w[...],
        gain[...],
    )
    out[...] = others[...]
    out[land] = y
    zeros = jnp.zeros((7, INNER), F32)

    def again(value):
        high = value.astype(BF).astype(F32)
        rest = value - high
        middle = rest.astype(BF).astype(F32)
        return high, middle, rest - middle

    kh, km, kl = again(keep)
    a1h, a1l, _ = again(a1)
    a2h, a2l, _ = again(a2)
    rows = jnp.concatenate([kh, km, kl, a1h, a1l, a1h, a2h, a2l, a2h, zeros], 0)
    columns = rows.T.astype(BF)
    b1h, b1l, _ = again(b1)
    b2h, b2l, _ = again(b2)
    none = jnp.zeros((3, STATE_N), F32)
    inner = jnp.concatenate(
        [none, b1h, b1h, b1l, b2h, b2h, b2l, jnp.zeros((7, STATE_N), F32)], 0
    ).astype(BF)
    row = lax.broadcasted_iota(jnp.int32, (16, 128), 0)
    ones = jnp.where(row < 3, 1.0, 0.0).astype(BF)
    kept = dot_nn(columns, ones)
    for half, part in enumerate((left, right)):
        added = dot_nn(columns, inner[:, half * 128 : half * 128 + 128])
        result = part.astype(F32) * kept + added
        final[0, :, :, half * 128 : half * 128 + 128] = result.astype(BF).reshape(HEADS, HEAD_P, 128)


def mixer_landed(idx, move_src, shares, fresh, gate, dt_raw, a_log, dt_bias, skip, conv_w, gain, others):
    return pl.pallas_call(
        mixer_landed_kernel,
        out_shape=(
            jax.ShapeDtypeStruct((SLOTS, 2, INNER), BF),
            jax.ShapeDtypeStruct((1, HEADS, HEAD_P, STATE_N), BF),
        ),
        in_specs=[SMEM, SMEM] + [VMEM] * 10,
        out_specs=(VMEM, VMEM),
        compiler_params=params(),
        cost_estimate=cost(5),
    )(idx, move_src, shares, fresh, gate, dt_raw, a_log, dt_bias, skip, conv_w, gain, others)


def attend(queries, keys, values, new_kv, length, flip):
    q = queries.astype(F32)
    q_rows = jnp.concatenate([q[:, h * 128 : h * 128 + 128] for h in range(8)], 0).astype(BF)
    fresh = new_kv.astype(F32)
    pad = jnp.zeros((TOK - 2, 128), F32)
    new_keys = jnp.concatenate([fresh[0, 0:1], fresh[1, 0:1], pad], 0).astype(BF)
    new_values = jnp.concatenate([fresh[0, 1:2], fresh[1, 1:2], pad], 0).astype(BF)
    cached = PPR * TP * TOK
    all_keys = jnp.concatenate(keys + [new_keys], 0)
    all_values = jnp.concatenate(values + [new_values], 0)
    scores = dot_nt(q_rows, all_keys) * (HEAD_D**-0.5)
    shape = (16, cached + TOK)
    column = lax.broadcasted_iota(jnp.int32, shape, 1)
    step = lax.broadcasted_iota(jnp.int32, shape, 0) & 1
    held = (column >> 4) & (TP - 1)
    position = (column & ~127) + ((held ^ flip) << 4) + (column & 15)
    allowed = jnp.where(column < cached, position - length, column - cached - step - 1) < 0
    peak = jnp.max(jnp.where(allowed, scores, -1e30), -1, keepdims=True)
    weights = jnp.where(allowed, jnp.exp(scores - peak), 0.0)
    total = jnp.sum(weights, -1, keepdims=True)
    high, low = halves(weights)
    out = (dot_nn(high, all_values) + dot_nn(low, all_values)) / total
    return jnp.concatenate([out[2 * h : 2 * h + 2] for h in range(8)], 1).astype(BF)


def attend_all_kernel(idx, table, lengths, queries, new_kv, *refs):
    pieces, out = refs[:TP], refs[TP]

    def one(slot, carry):
        keys, values = [], []
        for page in range(PPR):
            at = table[page, slot]
            for d in range(TP):
                keys.append(pieces[d][at, 0])
                values.append(pieces[d][at, 1])
        length = lengths[idx[0] * SLOTS + slot]
        out[slot] = attend(queries[slot], keys, values, new_kv[slot], length, idx[1])
        return carry

    lax.fori_loop(0, SLOTS, one, 0)


def attend_all(idx, table, lengths, queries, new_kv, pieces):
    return pl.pallas_call(
        attend_all_kernel,
        out_shape=jax.ShapeDtypeStruct(queries.shape, BF),
        in_specs=[SMEM, SMEM, SMEM] + [VMEM] * (2 + TP),
        out_specs=VMEM,
        compiler_params=params(),
        cost_estimate=cost(8),
    )(idx, table, lengths, queries, new_kv, *pieces)


def attend_landed_kernel(idx, move_src, move_dst, lengths, queries, new_kv, pages, others, out):
    here = move_src[idx[0]]
    land = here & (SLOTS - 1)

    def seek(j, found):
        return jnp.where(move_dst[j] == here, move_src[j], found)

    origin = lax.fori_loop(0, N_INST, seek, jnp.int32(0))
    keys = [pages[r, 2 * p] for p in range(PPR) for r in range(TP)]
    values = [pages[r, 2 * p + 1] for p in range(PPR) for r in range(TP)]
    result = attend(queries[land], keys, values, new_kv[land], lengths[origin], 0)
    out[...] = others[...]
    out[land] = result


def attend_landed(idx, move_src, move_dst, lengths, queries, new_kv, pages, others):
    return pl.pallas_call(
        attend_landed_kernel,
        out_shape=jax.ShapeDtypeStruct(queries.shape, BF),
        in_specs=[SMEM] * 4 + [VMEM] * 4,
        out_specs=VMEM,
        compiler_params=params(),
        cost_estimate=cost(2),
    )(idx, move_src, move_dst, lengths, queries, new_kv, pages, others)


def shards(
    ssm_state,
    conv_tail,
    kv_pool,
    page_table,
    lengths,
    move_src,
    move_dst,
    x_in,
    z_gate,
    dt_raw,
    queries,
    new_kv,
    a_log,
    dt_bias,
    skip_d,
    conv_w,
    norm_gain,
):
    idx = jnp.stack([lax.axis_index("inst"), lax.axis_index("tp")]).astype(jnp.int32)
    tail = jnp.transpose(conv_tail, (1, 0, 2))
    table = jnp.transpose(page_table, (1, 0))
    a_row, bias_row, skip_row = a_log[None], dt_bias[None], skip_d[None]
    gain_row = norm_gain[None]

    packed = pack(idx, move_src, table, ssm_state, tail, kv_pool)
    spread = lax.all_to_all(packed, "inst", 0, 0, tiled=True)

    pieces = split_heads(idx, kv_pool)
    pieces = [pieces[0]] + [
        lax.ppermute(pieces[d], "tp", [(i, i ^ d) for i in range(TP)]) for d in range(1, TP)
    ]
    mixed = mixer_all(
        ssm_state, tail, x_in, z_gate, dt_raw, a_row, bias_row, skip_row, conv_w, gain_row
    )
    shares = reorder(move_dst, spread)
    landed = lax.all_to_all(shares, "inst", 0, 0, tiled=True)
    attended = attend_all(idx, table, lengths, queries, new_kv, pieces)

    arrived_pages, send = unpack(landed)
    pages = lax.all_to_all(send, "tp", 0, 0, tiled=True)
    mamba_out, arrived_state = mixer_landed(
        idx, move_src, landed, x_in, z_gate, dt_raw, a_row, bias_row, skip_row, conv_w, gain_row, mixed
    )
    attn_out = attend_landed(idx, move_src, move_dst, lengths, queries, new_kv, pages, attended)
    return mamba_out, attn_out, arrived_state, arrived_pages


def solution(mesh):
    in_specs = (
        P("inst", "tp", None, None),
        P("inst", None, "tp"),
        P("inst", None, "tp", None),
        P("inst", None),
        P(),
        P(),
        P(),
        P("inst", None, "tp"),
        P("inst", None, "tp"),
        P("inst", None, "tp"),
        P("inst", None, "tp"),
        P("inst", None, None, "tp"),
        P("tp"),
        P("tp"),
        P("tp"),
        P(None, "tp"),
        P("tp"),
    )
    out_specs = (
        P("inst", None, "tp"),
        P("inst", None, "tp"),
        P("inst", "tp", None, None),
        P("inst", None, "tp", None),
    )
    return jax.shard_map(shards, mesh=mesh, in_specs=in_specs, out_specs=out_specs, check_vma=False)
```

```python
import functools

import jax
import jax.numpy as jnp
from jax import lax
from jax.experimental import pallas as pl
from jax.experimental.pallas import tpu as pltpu
from jax.sharding import PartitionSpec as P

BF = jnp.bfloat16
F32 = jnp.float32
HEADS = 32
HEAD_P = 64
INNER = 2048
STATE_N = 256
CONV = 2560
HEAD_D = 128
PAGE = 128
PPR = 4
TP = 8
TOK = 16
N_INST = 32
SLOTS = 8
PAGE_AT = 128
TAIL_AT = 160
NEW_AT = 162
HEAD_AT = 168
ROWS = 184
TAIL_ROWS = 60

SMEM = pl.BlockSpec(memory_space=pltpu.SMEM)
VMEM = pl.BlockSpec(memory_space=pltpu.VMEM)
ANY = pl.BlockSpec(memory_space=pl.ANY)
HBM = pl.BlockSpec(memory_space=pltpu.HBM)


def params():
    return pltpu.CompilerParams(vmem_limit_bytes=48 * 1024 * 1024)


def cost(microseconds):
    return pl.CostEstimate(
        flops=int(microseconds * 5e8), bytes_accessed=int(microseconds * 3e6), transcendentals=0
    )


def halves(value):
    high = value.astype(BF)
    low = (value - high.astype(F32)).astype(BF)
    return high, low


def thirds(value):
    high = value.astype(BF)
    rest = value - high.astype(F32)
    middle = rest.astype(BF)
    low = (rest - middle.astype(F32)).astype(BF)
    return high, middle, low


def dot_nt(left, right):
    return lax.dot_general(left, right, (((1,), (1,)), ((), ())), preferred_element_type=F32)


def dot_nn(left, right):
    return lax.dot_general(left, right, (((1,), (0,)), ((), ())), preferred_element_type=F32)


def head_rows(value):
    return jnp.concatenate([value[:, h * 128 : h * 128 + 128] for h in range(8)], 0)


def pack_kernel(
    move_src,
    table,
    state,
    tail,
    pool,
    queries,
    new_kv,
    out,
    src_s,
    table_s,
    tail_v,
    queries_v,
    new_v,
    pages,
    tail_rows,
    sems,
    page_sems,
):
    early = [
        pltpu.make_async_copy(move_src, src_s, sems.at[0]),
        pltpu.make_async_copy(table, table_s, sems.at[1]),
        pltpu.make_async_copy(tail, tail_v, sems.at[2]),
        pltpu.make_async_copy(queries, queries_v, sems.at[3]),
        pltpu.make_async_copy(new_kv, new_v, sems.at[4]),
    ]
    for copy in early:
        copy.start()
    early[0].wait()
    leave = src_s[lax.axis_index("inst")] & (SLOTS - 1)
    states = [
        pltpu.make_async_copy(
            state.at[leave, :, :, pl.ds(half * 128, 128)],
            out.at[:, pl.ds(half * 64, 64), :],
            sems.at[5 + half],
        )
        for half in range(2)
    ]
    for copy in states:
        copy.start()
    early[1].wait()
    page_copies = [
        pltpu.make_async_copy(pool.at[table_s[page, leave]], pages.at[page], page_sems.at[page])
        for page in range(PPR)
    ]
    for copy in page_copies:
        copy.start()
    for copy in early[2:]:
        copy.wait()
    rows = head_rows(queries_v[leave].astype(F32)).astype(BF)
    out[:, HEAD_AT:ROWS, :] = jnp.broadcast_to(rows[None], (N_INST, 16, 128))
    fresh = new_v[leave].astype(F32)
    tail_rows[...] = jnp.zeros_like(tail_rows)
    for u in range(2):
        tail_rows[:, 2 + 2 * u : 4 + 2 * u, :] = jnp.broadcast_to(fresh[u][None], (N_INST, 2, 128))
    slot = lax.broadcasted_iota(jnp.int32, (3, SLOTS, CONV), 1)
    mine = jnp.sum(jnp.where(slot == leave, tail_v[...].astype(F32), 0.0), 1)
    for row in range(TAIL_ROWS):
        tap, at = row // 20, (row % 20) * 128
        tail_rows[row // 2, row % 2 : row % 2 + 1, :] = mine[tap : tap + 1, at : at + 128]
    out[:, TAIL_AT:HEAD_AT, :] = tail_rows[...].astype(BF)
    for copy in page_copies:
        copy.wait()
    for kv in range(2 * PPR):
        for head in range(TP):
            at = PAGE_AT + TOK * (head % 2)
            out[kv * 4 + head // 2, at : at + TOK, :] = pages[
                kv // 2, kv % 2, :, head * 128 : head * 128 + 128
            ]
    for copy in states:
        copy.wait()


def pack(move_src, table, state, tail, pool, queries, new_kv):
    return pl.pallas_call(
        pack_kernel,
        out_shape=jax.ShapeDtypeStruct((N_INST, ROWS, 128), BF),
        in_specs=[ANY] * 7,
        out_specs=VMEM,
        scratch_shapes=[
            pltpu.SMEM(move_src.shape, jnp.int32),
            pltpu.SMEM(table.shape, jnp.int32),
            pltpu.VMEM(tail.shape, BF),
            pltpu.VMEM(queries.shape, BF),
            pltpu.VMEM(new_kv.shape, BF),
            pltpu.VMEM((PPR, 2, TOK, TP * 128), BF),
            pltpu.VMEM((N_INST, 8, 128), F32),
            pltpu.SemaphoreType.DMA((7,)),
            pltpu.SemaphoreType.DMA((PPR,)),
        ],
        cost_estimate=cost(3),
    )(move_src, table, state, tail, pool, queries, new_kv)


def turn_kernel(move_src, move_dst, table, lengths, shares, *refs):
    pairs, (out, held, sems) = refs[: TP // 2], refs[TP // 2 :]
    inst, me = lax.axis_index("inst"), lax.axis_index("tp")
    leaving = move_src[inst]
    leave = leaving & (SLOTS - 1)
    copies = []
    for page in range(PPR):
        at = 2 * table[page, leave]
        for e in range(TP // 2):
            copies.append(
                pltpu.make_async_copy(
                    pairs[e].at[:, pl.ds(at, 2)], held.at[page, e], sems.at[page * (TP // 2) + e]
                )
            )
    for copy in copies:
        copy.start()

    def turn(j, carry):
        out[move_dst[j] >> 3, 0:HEAD_AT, :] = shares[j, 0:HEAD_AT, :]
        return carry

    lax.fori_loop(0, N_INST, turn, 0)
    target = move_dst[inst] >> 3
    q_rows = shares[target, HEAD_AT:ROWS, :]
    fresh = shares[target, TAIL_AT:HEAD_AT, :].astype(F32)
    for copy in copies:
        copy.wait()
    keys = [held[p, d // 2, d % 2, 0] for p in range(PPR) for d in range(TP)]
    values = [held[p, d // 2, d % 2, 1] for p in range(PPR) for d in range(TP)]
    new_keys = jnp.concatenate([fresh[2:3], fresh[4:5]], 0)
    new_values = jnp.concatenate([fresh[3:4], fresh[5:6]], 0)
    rows = attend(q_rows, keys, values, new_keys, new_values, lengths[leaving], me)
    out[target, HEAD_AT:ROWS, :] = rows.astype(BF)


def turn(move_src, move_dst, table, lengths, shares, pairs):
    return pl.pallas_call(
        turn_kernel,
        out_shape=jax.ShapeDtypeStruct(shares.shape, BF),
        in_specs=[SMEM] * 4 + [VMEM] + [ANY] * (TP // 2),
        out_specs=VMEM,
        scratch_shapes=[
            pltpu.VMEM((PPR, TP // 2, 2, 2, TOK, 128), BF),
            pltpu.SemaphoreType.DMA((PPR * TP // 2,)),
        ],
        compiler_params=params(),
        cost_estimate=cost(3),
    )(move_src, move_dst, table, lengths, shares, *pairs)


def split_heads_kernel(pool, own, other, sems):
    me = lax.axis_index("tp")
    copies = []
    for e in range(TP // 2):
        for b, ref in enumerate((own, other)):
            at = pl.multiple_of((me ^ (2 * e + b)) * 128, 128)
            copies.append(
                pltpu.make_async_copy(pool.at[:, :, pl.ds(at, 128)], ref.at[e], sems.at[2 * e + b])
            )
    for copy in copies:
        copy.start()
    for copy in copies:
        copy.wait()


def split_heads(pool):
    part = jax.ShapeDtypeStruct((TP // 2,) + pool.shape[:2] + (128,), BF)
    return pl.pallas_call(
        split_heads_kernel,
        out_shape=(part, part),
        in_specs=[ANY],
        out_specs=(ANY, ANY),
        scratch_shapes=[pltpu.SemaphoreType.DMA((TP,))],
        compiler_params=params(),
        cost_estimate=cost(2),
    )(pool)


def pair_kernel(own, other, *refs):
    outs, sems = refs[: TP // 2], refs[TP // 2]
    copies = []
    for e in range(TP // 2):
        for b, ref in enumerate((own, other)):
            copies.append(pltpu.make_async_copy(ref.at[e], outs[e].at[b], sems.at[2 * e + b]))
    for copy in copies:
        copy.start()
    for copy in copies:
        copy.wait()


def exchange(own, other):
    swapped = lax.ppermute(other, "tp", [(i, i ^ 1) for i in range(TP)])
    pair = jax.ShapeDtypeStruct((2,) + own.shape[1:], BF)
    pairs = pl.pallas_call(
        pair_kernel,
        out_shape=(pair,) * (TP // 2),
        in_specs=[ANY, ANY],
        out_specs=(ANY,) * (TP // 2),
        scratch_shapes=[pltpu.SemaphoreType.DMA((TP,))],
        compiler_params=params(),
        cost_estimate=cost(1),
    )(own, swapped)
    return [pairs[0]] + [
        lax.ppermute(pairs[e], "tp", [(i, i ^ (2 * e)) for i in range(TP)]) for e in range(1, TP // 2)
    ]


def silu(value):
    return value * (1.0 / (1.0 + jnp.exp(-value)))


def mixer(state_dots, tail, fresh, gate, dt_raw, a_log, dt_bias, skip, conv_w, gain):
    window = [tail[k : k + 1] for k in range(3)] + [fresh[k : k + 1] for k in range(2)]
    steps = []
    for t in range(2):
        total = conv_w[0:1] * window[t]
        for k in range(1, 4):
            total = total + conv_w[k : k + 1] * window[t + k]
        steps.append(total)
    conv = silu(jnp.concatenate(steps, 0))
    x = conv[:, :INNER]
    b_in = conv[:, INNER : INNER + STATE_N]
    c_out = conv[:, INNER + STATE_N :]

    raw = dt_raw + dt_bias
    step = jnp.maximum(raw, 0.0) + jnp.log1p(jnp.exp(-jnp.abs(raw)))
    retain = jnp.exp(-step * jnp.exp(a_log))
    per_head = jnp.concatenate([step, retain, skip, jnp.zeros((3, HEADS), F32)], 0)
    head_row = lax.broadcasted_iota(jnp.int32, (HEADS, INNER), 0)
    channel = lax.broadcasted_iota(jnp.int32, (HEADS, INNER), 1)
    spread = jnp.where(channel // HEAD_P == head_row, 1.0, 0.0).astype(BF)
    spread_out = sum(dot_nn(part, spread) for part in thirds(per_head))
    step1, step2 = spread_out[0:1], spread_out[1:2]
    keep1, keep2 = spread_out[2:3], spread_out[3:4]
    skip_c = spread_out[4:5]

    c_high, c_low = halves(c_out)
    dots = state_dots(jnp.concatenate([c_high, c_low, jnp.zeros((12, STATE_N), BF)], 0))
    dots = dots[0:2] + dots[2:4]
    b1, b2, c1, c2 = b_in[0:1], b_in[1:2], c_out[0:1], c_out[1:2]
    x1, x2 = x[0:1], x[1:2]
    u1, u2 = step1 * x1, step2 * x2
    bc11 = jnp.sum(b1 * c1, -1, keepdims=True)
    bc12 = jnp.sum(b1 * c2, -1, keepdims=True)
    bc22 = jnp.sum(b2 * c2, -1, keepdims=True)
    y1 = keep1 * dots[0:1] + u1 * bc11 + skip_c * x1
    y2 = keep2 * (keep1 * dots[1:2] + u1 * bc12) + u2 * bc22 + skip_c * x2
    y = jnp.concatenate([y1, y2], 0) * silu(gate)
    y = y * lax.rsqrt(jnp.mean(y * y, -1, keepdims=True) + 1e-05) * gain
    return y.astype(BF), (keep2 * u1, u2, b1, b2, keep1 * keep2)


def mixer_all_kernel(state, tail, fresh, gate, dt_raw, a_log, dt_bias, skip, conv_w, gain, out):
    here = pl.program_id(0)
    slot = lax.broadcasted_iota(jnp.int32, (3, SLOTS, CONV), 1)
    mine = jnp.sum(jnp.where(slot == here, tail[...].astype(F32), 0.0), 1)
    rows = state[0].reshape(INNER, STATE_N)
    y, _ = mixer(
        lambda lhs: dot_nt(lhs, rows),
        mine,
        fresh[0].astype(F32),
        gate[0].astype(F32),
        dt_raw[0],
        a_log[...],
        dt_bias[...],
        skip[...],
        conv_w[...],
        gain[...],
    )
    out[0] = y


def mixer_all(state, tail, fresh, gate, dt_raw, a_log, dt_bias, skip, conv_w, gain):
    def whole(shape):
        return pl.BlockSpec(shape, lambda s: (0,) * len(shape))

    def by_slot(shape):
        return pl.BlockSpec((1,) + shape, lambda s: (s,) + (0,) * len(shape))

    return pl.pallas_call(
        mixer_all_kernel,
        grid=(SLOTS,),
        out_shape=jax.ShapeDtypeStruct((SLOTS, 2, INNER), BF),
        in_specs=[
            by_slot((HEADS, HEAD_P, STATE_N)),
            whole((3, SLOTS, CONV)),
            by_slot((2, CONV)),
            by_slot((2, INNER)),
            by_slot((2, HEADS)),
            whole((1, HEADS)),
            whole((1, HEADS)),
            whole((1, HEADS)),
            whole((4, CONV)),
            whole((1, INNER)),
        ],
        out_specs=by_slot((2, INNER)),
        compiler_params=params(),
        cost_estimate=cost(16),
    )(state, tail, fresh, gate, dt_raw, a_log, dt_bias, skip, conv_w, gain)


def landed_kernel(
    move_src,
    move_dst,
    shares,
    fresh,
    gate,
    dt_raw,
    a_log,
    dt_bias,
    skip,
    conv_w,
    gain,
    mixed,
    attended,
    out,
    attn_out,
    final,
    arrived,
):
    here = move_src[lax.axis_index("inst")]
    land = here & (SLOTS - 1)

    def seek(j, found):
        return jnp.where(move_dst[j] == here, j, found)

    origin = lax.fori_loop(0, N_INST, seek, jnp.int32(0))
    rows = shares[origin, HEAD_AT:ROWS, :].astype(F32)
    attn_out[...] = attended[...]
    attn_out[land] = jnp.concatenate([rows[2 * h : 2 * h + 2] for h in range(8)], 1).astype(BF)
    for kv in range(2 * PPR):
        for head in range(TP):
            at = PAGE_AT + TOK * (head % 2)
            arrived[kv // 2, kv % 2, :, head * 128 : head * 128 + 128] = shares[
                kv * 4 + head // 2, at : at + TOK, :
            ]
    pieces = shares[:, TAIL_AT:HEAD_AT, :].astype(F32)
    tail = jnp.concatenate(
        [
            jnp.concatenate(
                [pieces[row // 2, row % 2 : row % 2 + 1, :] for row in range(tap * 20, tap * 20 + 20)], 1
            )
            for tap in range(3)
        ],
        0,
    )
    left = shares[:, 0:64, :].reshape(INNER, 128)
    right = shares[:, 64:128, :].reshape(INNER, 128)
    y, (a1, a2, b1, b2, keep) = mixer(
        lambda lhs: dot_nt(lhs[:, :128], left) + dot_nt(lhs[:, 128:], right),
        tail,
        fresh[land].astype(F32),
        gate[land].astype(F32),
        dt_raw[land],
        a_log[...],
        dt_bias[...],
        skip[...],
        conv_w[...],
        gain[...],
    )
    out[...] = mixed[...]
    out[land] = y
    zeros = jnp.zeros((7, INNER), F32)

    def again(value):
        high = value.astype(BF).astype(F32)
        rest = value - high
        middle = rest.astype(BF).astype(F32)
        return high, middle, rest - middle

    kh, km, kl = again(keep)
    a1h, a1l, _ = again(a1)
    a2h, a2l, _ = again(a2)
    rows = jnp.concatenate([kh, km, kl, a1h, a1l, a1h, a2h, a2l, a2h, zeros], 0)
    columns = rows.T.astype(BF)
    b1h, b1l, _ = again(b1)
    b2h, b2l, _ = again(b2)
    none = jnp.zeros((3, STATE_N), F32)
    inner = jnp.concatenate(
        [none, b1h, b1h, b1l, b2h, b2h, b2l, jnp.zeros((7, STATE_N), F32)], 0
    ).astype(BF)
    row = lax.broadcasted_iota(jnp.int32, (16, 128), 0)
    ones = jnp.where(row < 3, 1.0, 0.0).astype(BF)
    kept = dot_nn(columns, ones)
    for half, part in enumerate((left, right)):
        added = dot_nn(columns, inner[:, half * 128 : half * 128 + 128])
        result = part.astype(F32) * kept + added
        final[0, :, :, half * 128 : half * 128 + 128] = result.astype(BF).reshape(HEADS, HEAD_P, 128)


def landed(move_src, move_dst, shares, small, mixed, attended):
    return pl.pallas_call(
        landed_kernel,
        out_shape=(
            jax.ShapeDtypeStruct(mixed.shape, BF),
            jax.ShapeDtypeStruct(attended.shape, BF),
            jax.ShapeDtypeStruct((1, HEADS, HEAD_P, STATE_N), BF),
            jax.ShapeDtypeStruct((PPR, 2, TOK, TP * 128), BF),
        ),
        in_specs=[SMEM] * 2 + [VMEM] * 11,
        out_specs=(VMEM,) * 4,
        compiler_params=params(),
        cost_estimate=cost(4),
    )(move_src, move_dst, shares, *small, mixed, attended)


def attend(q_rows, keys, values, new_keys, new_values, length, flip):
    pad = jnp.zeros((TOK - 2, 128), F32)
    new_keys = jnp.concatenate([new_keys, pad], 0).astype(BF)
    new_values = jnp.concatenate([new_values, pad], 0).astype(BF)
    cached = PPR * TP * TOK
    all_keys = jnp.concatenate(keys + [new_keys], 0)
    all_values = jnp.concatenate(values + [new_values], 0)
    scores = dot_nt(q_rows, all_keys) * (HEAD_D**-0.5)
    shape = (16, cached + TOK)
    column = lax.broadcasted_iota(jnp.int32, shape, 1)
    step = lax.broadcasted_iota(jnp.int32, shape, 0) & 1
    held = (column >> 4) & (TP - 1)
    position = (column & ~127) + ((held ^ flip) << 4) + (column & 15)
    allowed = jnp.where(column < cached, position - length, column - cached - step - 1) < 0
    peak = jnp.max(jnp.where(allowed, scores, -1e30), -1, keepdims=True)
    weights = jnp.where(allowed, jnp.exp(scores - peak), 0.0)
    total = jnp.sum(weights, -1, keepdims=True)
    high, low = halves(weights)
    return (dot_nn(high, all_values) + dot_nn(low, all_values)) / total


def attend_all_kernel(table, lengths, queries, new_kv, *refs):
    pairs, out = refs[: TP // 2], refs[TP // 2]
    inst, me = lax.axis_index("inst"), lax.axis_index("tp")

    def one(slot, carry):
        keys, values = [], []
        for page in range(PPR):
            at = table[page, slot]
            for d in range(TP):
                keys.append(pairs[d // 2][d % 2, 2 * at])
                values.append(pairs[d // 2][d % 2, 2 * at + 1])
        length = lengths[inst * SLOTS + slot]
        q_rows = head_rows(queries[slot].astype(F32)).astype(BF)
        fresh = new_kv[slot].astype(F32)
        rows = attend(q_rows, keys, values, fresh[:, 0], fresh[:, 1], length, me)
        out[slot] = jnp.concatenate([rows[2 * h : 2 * h + 2] for h in range(8)], 1).astype(BF)
        return carry

    lax.fori_loop(0, SLOTS, one, 0)


def attend_all(table, lengths, queries, new_kv, pairs):
    return pl.pallas_call(
        attend_all_kernel,
        out_shape=jax.ShapeDtypeStruct(queries.shape, BF),
        in_specs=[SMEM, SMEM] + [VMEM] * (2 + TP // 2),
        out_specs=VMEM,
        compiler_params=params(),
        cost_estimate=cost(4),
    )(table, lengths, queries, new_kv, *pairs)


def shards(
    ssm_state,
    conv_tail,
    kv_pool,
    page_table,
    lengths,
    move_src,
    move_dst,
    x_in,
    z_gate,
    dt_raw,
    queries,
    new_kv,
    a_log,
    dt_bias,
    skip_d,
    conv_w,
    norm_gain,
):
    tail = jnp.transpose(conv_tail, (1, 0, 2))
    table = jnp.transpose(page_table, (1, 0))
    a_row, bias_row, skip_row = a_log[None], dt_bias[None], skip_d[None]
    gain_row = norm_gain[None]
    small = (x_in, z_gate, dt_raw, a_row, bias_row, skip_row, conv_w, gain_row)

    packed = pack(move_src, table, ssm_state, tail, kv_pool, queries, new_kv)
    spread = lax.all_to_all(packed, "inst", 0, 0, tiled=True)

    pool = kv_pool.reshape((-1,) + kv_pool.shape[2:])
    pairs = exchange(*split_heads(pool))
    mixed = mixer_all(ssm_state, tail, *small)
    spread, mixed, pairs = lax.optimization_barrier((spread, mixed, pairs))

    turned = turn(move_src, move_dst, table, lengths, spread, pairs)
    turned, pairs = lax.optimization_barrier((turned, pairs))
    shares = lax.all_to_all(turned, "inst", 0, 0, tiled=True)

    attended = attend_all(table, lengths, queries, new_kv, pairs)
    mamba_out, attn_out, arrived_state, arrived_pages = landed(
        move_src, move_dst, shares, small, mixed, attended
    )
    return mamba_out, attn_out, arrived_state, arrived_pages


def solution(mesh):
    in_specs = (
        P("inst", "tp", None, None),
        P("inst", None, "tp"),
        P("inst", None, "tp", None),
        P("inst", None),
        P(),
        P(),
        P(),
        P("inst", None, "tp"),
        P("inst", None, "tp"),
        P("inst", None, "tp"),
        P("inst", None, "tp"),
        P("inst", None, None, "tp"),
        P("tp"),
        P("tp"),
        P("tp"),
        P(None, "tp"),
        P("tp"),
    )
    out_specs = (
        P("inst", None, "tp"),
        P("inst", None, "tp"),
        P("inst", "tp", None, None),
        P("inst", None, "tp", None),
    )
    return jax.shard_map(shards, mesh=mesh, in_specs=in_specs, out_specs=out_specs, check_vma=False)
```

```python
import functools

import jax
import jax.numpy as jnp
from jax import lax
from jax.experimental import pallas as pl
from jax.experimental.pallas import tpu as pltpu
from jax.sharding import PartitionSpec as P

BF = jnp.bfloat16
F32 = jnp.float32
HEADS = 32
HEAD_P = 64
INNER = 2048
STATE_N = 256
CONV = 2560
HEAD_D = 128
PAGE = 128
PPR = 4
TP = 8
TOK = 16
N_INST = 32
SLOTS = 8
PAGE_AT = 128
HEAD_AT = 160
TAIL_AT = 176
ROWS_1 = 184
ROWS_2 = 176
TAIL_ROWS = 60

SMEM = pl.BlockSpec(memory_space=pltpu.SMEM)
VMEM = pl.BlockSpec(memory_space=pltpu.VMEM)
ANY = pl.BlockSpec(memory_space=pl.ANY)
HBM = pl.BlockSpec(memory_space=pltpu.HBM)


def params():
    return pltpu.CompilerParams(vmem_limit_bytes=48 * 1024 * 1024)


def cost(microseconds):
    return pl.CostEstimate(
        flops=int(microseconds * 5e8), bytes_accessed=int(microseconds * 3e6), transcendentals=0
    )


def in_hbm(value):
    return pltpu.with_memory_space_constraint(value, pltpu.HBM)


def halves(value):
    high = value.astype(BF)
    low = (value - high.astype(F32)).astype(BF)
    return high, low


def thirds(value):
    high = value.astype(BF)
    rest = value - high.astype(F32)
    middle = rest.astype(BF)
    low = (rest - middle.astype(F32)).astype(BF)
    return high, middle, low


def dot_nt(left, right):
    return lax.dot_general(left, right, (((1,), (1,)), ((), ())), preferred_element_type=F32)


def dot_nn(left, right):
    return lax.dot_general(left, right, (((1,), (0,)), ((), ())), preferred_element_type=F32)


def head_rows(value):
    return jnp.concatenate([value[:, h * 128 : h * 128 + 128] for h in range(8)], 0)


def pack_kernel(
    move_src,
    table,
    state,
    tail,
    pool,
    queries,
    new_kv,
    packed,
    out,
    src_s,
    table_s,
    tail_v,
    queries_v,
    new_v,
    pages,
    tail_rows,
    sems,
    page_sems,
    state_sems,
    out_sems,
):
    early = [
        pltpu.make_async_copy(move_src, src_s, sems.at[0]),
        pltpu.make_async_copy(table, table_s, sems.at[1]),
        pltpu.make_async_copy(tail, tail_v, sems.at[2]),
        pltpu.make_async_copy(queries, queries_v, sems.at[3]),
        pltpu.make_async_copy(new_kv, new_v, sems.at[4]),
    ]
    for copy in early:
        copy.start()
    early[0].wait()
    inst = lax.axis_index("inst")
    leave = src_s[inst] & (SLOTS - 1)
    parts = 4
    heads = HEADS // parts
    states = [
        pltpu.make_async_copy(
            state.at[leave, pl.ds(part * heads, heads), :, pl.ds(half * 128, 128)],
            out.at[pl.ds(part * heads, heads), pl.ds(half * 64, 64), :],
            state_sems.at[2 * part + half],
        )
        for part in range(parts)
        for half in range(2)
    ]
    for copy in states:
        copy.start()
    early[1].wait()
    page_copies = [
        pltpu.make_async_copy(pool.at[table_s[page, leave]], pages.at[page], page_sems.at[page])
        for page in range(PPR)
    ]
    for copy in page_copies:
        copy.start()
    for copy in early[2:]:
        copy.wait()
    rows = head_rows(queries_v[leave].astype(F32)).astype(BF)
    out[:, HEAD_AT:TAIL_AT, :] = jnp.broadcast_to(rows[None], (N_INST, 16, 128))
    fresh = new_v[leave].astype(F32)
    tail_rows[...] = jnp.zeros_like(tail_rows)
    for u in range(2):
        tail_rows[:, 2 + 2 * u : 4 + 2 * u, :] = jnp.broadcast_to(fresh[u][None], (N_INST, 2, 128))
    slot = lax.broadcasted_iota(jnp.int32, (3, SLOTS, CONV), 1)
    mine = jnp.sum(jnp.where(slot == leave, tail_v[...].astype(F32), 0.0), 1)
    for row in range(TAIL_ROWS):
        tap, at = row // 20, (row % 20) * 128
        holder = (inst + 1 + row // 2) & (N_INST - 1)
        tail_rows[holder, row % 2 : row % 2 + 1, :] = mine[tap : tap + 1, at : at + 128]
    out[:, TAIL_AT:ROWS_1, :] = tail_rows[...].astype(BF)
    for copy in page_copies:
        copy.wait()
    for kv in range(2 * PPR):
        for head in range(TP):
            at = PAGE_AT + TOK * (head % 2)
            out[kv * 4 + head // 2, at : at + TOK, :] = pages[
                kv // 2, kv % 2, :, head * 128 : head * 128 + 128
            ]
    sent = []
    for part in range(parts):
        states[2 * part].wait()
        states[2 * part + 1].wait()
        rows = pl.ds(part * heads, heads)
        sent.append(pltpu.make_async_copy(out.at[rows], packed.at[rows], out_sems.at[part]))
        sent[part].start()
    for copy in sent:
        copy.wait()


def pack(move_src, table, state, tail, pool, queries, new_kv):
    return pl.pallas_call(
        pack_kernel,
        out_shape=jax.ShapeDtypeStruct((N_INST, ROWS_1, 128), BF),
        in_specs=[ANY] * 7,
        out_specs=HBM,
        scratch_shapes=[
            pltpu.VMEM((N_INST, ROWS_1, 128), BF),
            pltpu.SMEM(move_src.shape, jnp.int32),
            pltpu.SMEM(table.shape, jnp.int32),
            pltpu.VMEM(tail.shape, BF),
            pltpu.VMEM(queries.shape, BF),
            pltpu.VMEM(new_kv.shape, BF),
            pltpu.VMEM((PPR, 2, TOK, TP * 128), BF),
            pltpu.VMEM((N_INST, 8, 128), F32),
            pltpu.SemaphoreType.DMA((5,)),
            pltpu.SemaphoreType.DMA((PPR,)),
            pltpu.SemaphoreType.DMA((8,)),
            pltpu.SemaphoreType.DMA((4,)),
        ],
        cost_estimate=cost(3),
    )(move_src, table, state, tail, pool, queries, new_kv)


def gather_kernel(move_src, table, *refs):
    pairs, (keys, values, held, sems) = refs[: TP // 2], refs[TP // 2 :]
    leave = move_src[lax.axis_index("inst")] & (SLOTS - 1)
    copies = []
    for page in range(PPR):
        at = 2 * table[page, leave]
        for e in range(TP // 2):
            copies.append(
                pltpu.make_async_copy(
                    pairs[e].at[:, pl.ds(at, 2)], held.at[page, e], sems.at[page * (TP // 2) + e]
                )
            )
    for copy in copies:
        copy.start()
    for copy in copies:
        copy.wait()
    for page in range(PPR):
        for d in range(TP):
            at = (page * TP + d) * TOK
            keys[at : at + TOK, :] = held[page, d // 2, d % 2, 0]
            values[at : at + TOK, :] = held[page, d // 2, d % 2, 1]


def gather(move_src, table, pairs):
    held = jax.ShapeDtypeStruct((PPR * TP * TOK, 128), BF)
    return pl.pallas_call(
        gather_kernel,
        out_shape=(held, held),
        in_specs=[SMEM] * 2 + [ANY] * (TP // 2),
        out_specs=(VMEM, VMEM),
        scratch_shapes=[
            pltpu.VMEM((PPR, TP // 2, 2, 2, TOK, 128), BF),
            pltpu.SemaphoreType.DMA((PPR * TP // 2,)),
        ],
        compiler_params=params(),
        cost_estimate=cost(1),
    )(move_src, table, *pairs)


def turn_kernel(move_src, move_dst, lengths, shares, keys, values, out, rest, slab_sems, rest_sem):
    inst, me = lax.axis_index("inst"), lax.axis_index("tp")
    slabs = [
        pltpu.make_async_copy(
            shares.at[j, pl.ds(0, HEAD_AT), :],
            out.at[move_dst[j] >> 3, pl.ds(0, HEAD_AT), :],
            slab_sems.at[j],
        )
        for j in range(N_INST)
    ]
    for slab in slabs:
        slab.start()
    for j in range(N_INST):
        rest[move_dst[j] >> 3, 0:8, :] = shares[j, TAIL_AT:ROWS_1, :]
    target = move_dst[inst] >> 3
    q_rows = shares[target, HEAD_AT:TAIL_AT, :]
    fresh = shares[target, TAIL_AT:ROWS_1, :].astype(F32)
    new_keys = jnp.concatenate([fresh[2:3], fresh[4:5]], 0)
    new_values = jnp.concatenate([fresh[3:4], fresh[5:6]], 0)
    length = lengths[move_src[inst]]
    rows = attend(q_rows, [keys[...]], [values[...]], new_keys, new_values, length, me)
    rest[target] = rows.astype(BF)
    last = pltpu.make_async_copy(rest, out.at[:, pl.ds(HEAD_AT, 16), :], rest_sem.at[0])
    last.start()
    for slab in slabs:
        slab.wait()
    last.wait()


def turn(move_src, move_dst, lengths, shares, keys, values):
    return pl.pallas_call(
        turn_kernel,
        out_shape=jax.ShapeDtypeStruct((N_INST, ROWS_2, 128), BF),
        in_specs=[SMEM] * 3 + [VMEM] * 3,
        out_specs=HBM,
        scratch_shapes=[
            pltpu.VMEM((N_INST, 16, 128), BF),
            pltpu.SemaphoreType.DMA((N_INST,)),
            pltpu.SemaphoreType.DMA((1,)),
        ],
        compiler_params=params(),
        cost_estimate=cost(3),
    )(move_src, move_dst, lengths, shares, keys, values)


def split_heads_kernel(pool, own, other, sems):
    me = lax.axis_index("tp")
    copies = []
    for e in range(TP // 2):
        for b, ref in enumerate((own, other)):
            at = pl.multiple_of((me ^ (2 * e + b)) * 128, 128)
            copies.append(
                pltpu.make_async_copy(pool.at[:, :, pl.ds(at, 128)], ref.at[e], sems.at[2 * e + b])
            )
    for copy in copies:
        copy.start()
    for copy in copies:
        copy.wait()


def split_heads(pool):
    part = jax.ShapeDtypeStruct((TP // 2,) + pool.shape[:2] + (128,), BF)
    return pl.pallas_call(
        split_heads_kernel,
        out_shape=(part, part),
        in_specs=[ANY],
        out_specs=(ANY, ANY),
        scratch_shapes=[pltpu.SemaphoreType.DMA((TP,))],
        compiler_params=params(),
        cost_estimate=cost(2),
    )(pool)


def pair_kernel(own, other, *refs):
    outs, sems = refs[: TP // 2], refs[TP // 2]
    copies = []
    for e in range(TP // 2):
        for b, ref in enumerate((own, other)):
            copies.append(pltpu.make_async_copy(ref.at[e], outs[e].at[b], sems.at[2 * e + b]))
    for copy in copies:
        copy.start()
    for copy in copies:
        copy.wait()


def exchange(own, other):
    swapped = lax.ppermute(other, "tp", [(i, i ^ 1) for i in range(TP)])
    pair = jax.ShapeDtypeStruct((2,) + own.shape[1:], BF)
    pairs = pl.pallas_call(
        pair_kernel,
        out_shape=(pair,) * (TP // 2),
        in_specs=[ANY, ANY],
        out_specs=(ANY,) * (TP // 2),
        scratch_shapes=[pltpu.SemaphoreType.DMA((TP,))],
        compiler_params=params(),
        cost_estimate=cost(1),
    )(own, swapped)
    return [pairs[0]] + [
        lax.ppermute(pairs[e], "tp", [(i, i ^ (2 * e)) for i in range(TP)]) for e in range(1, TP // 2)
    ]


def silu(value):
    return value * (1.0 / (1.0 + jnp.exp(-value)))


def convolve(tail, fresh, conv_w):
    window = [tail[k : k + 1] for k in range(3)] + [fresh[k : k + 1] for k in range(2)]
    steps = []
    for t in range(2):
        total = conv_w[0:1] * window[t]
        for k in range(1, 4):
            total = total + conv_w[k : k + 1] * window[t + k]
        steps.append(total)
    return silu(jnp.concatenate(steps, 0))


def per_channel(dt_raw, a_log, dt_bias, skip):
    raw = dt_raw + dt_bias
    step = jnp.maximum(raw, 0.0) + jnp.log1p(jnp.exp(-jnp.abs(raw)))
    retain = jnp.exp(-step * jnp.exp(a_log))
    per_head = jnp.concatenate([step, retain, skip, jnp.zeros((3, HEADS), F32)], 0)
    head_row = lax.broadcasted_iota(jnp.int32, (HEADS, INNER), 0)
    channel = lax.broadcasted_iota(jnp.int32, (HEADS, INNER), 1)
    spread = jnp.where(channel // HEAD_P == head_row, 1.0, 0.0).astype(BF)
    rows = sum(dot_nn(part, spread) for part in thirds(per_head))
    return [rows[k : k + 1] for k in range(5)]


def mixer(state_dots, conv, scales, gate, gain):
    b_in = conv[:, INNER : INNER + STATE_N]
    c_out = conv[:, INNER + STATE_N :]
    step1, step2, keep1, keep2, skip_c = scales
    c_high, c_low = halves(c_out)
    dots = state_dots(jnp.concatenate([c_high, c_low, jnp.zeros((12, STATE_N), BF)], 0))
    dots = dots[0:2] + dots[2:4]
    b1, b2, c1, c2 = b_in[0:1], b_in[1:2], c_out[0:1], c_out[1:2]
    x1, x2 = conv[0:1, :INNER], conv[1:2, :INNER]
    u1, u2 = step1 * x1, step2 * x2
    bc11 = jnp.sum(b1 * c1, -1, keepdims=True)
    bc12 = jnp.sum(b1 * c2, -1, keepdims=True)
    bc22 = jnp.sum(b2 * c2, -1, keepdims=True)
    y1 = keep1 * dots[0:1] + u1 * bc11 + skip_c * x1
    y2 = keep2 * (keep1 * dots[1:2] + u1 * bc12) + u2 * bc22 + skip_c * x2
    y = jnp.concatenate([y1, y2], 0) * gate
    y = y * lax.rsqrt(jnp.mean(y * y, -1, keepdims=True) + 1e-05) * gain
    return y.astype(BF)


def mixer_all_kernel(
    move_src, state, tail, fresh, gate, dt_raw, a_log, dt_bias, skip, conv_w, gain, out, kept
):
    here = pl.program_id(0)
    slot = lax.broadcasted_iota(jnp.int32, (3, SLOTS, CONV), 1)
    mine = jnp.sum(jnp.where(slot == here, tail[...].astype(F32), 0.0), 1)
    rows = state[0].reshape(INNER, STATE_N)
    new = fresh[0].astype(F32)
    scales = per_channel(dt_raw[0], a_log[...], dt_bias[...], skip[...])
    gated = silu(gate[0].astype(F32))
    out[0] = mixer(
        lambda lhs: dot_nt(lhs, rows), convolve(mine, new, conv_w[...]), scales, gated, gain[...]
    )

    @pl.when(here == (move_src[lax.axis_index("inst")] & (SLOTS - 1)))
    def _():
        kept[0:2, :] = new
        kept[2:6, :] = conv_w[...]
        for k in range(5):
            kept[6 + k : 7 + k, 0:INNER] = scales[k]
        kept[11:13, 0:INNER] = gated
        kept[13:14, 0:INNER] = gain[...]


def mixer_all(move_src, state, tail, fresh, gate, dt_raw, a_log, dt_bias, skip, conv_w, gain):
    def whole(shape):
        return pl.BlockSpec(shape, lambda s: (0,) * len(shape))

    def by_slot(shape):
        return pl.BlockSpec((1,) + shape, lambda s: (s,) + (0,) * len(shape))

    return pl.pallas_call(
        mixer_all_kernel,
        grid=(SLOTS,),
        out_shape=(
            jax.ShapeDtypeStruct((SLOTS, 2, INNER), BF),
            jax.ShapeDtypeStruct((16, CONV), F32),
        ),
        in_specs=[
            SMEM,
            by_slot((HEADS, HEAD_P, STATE_N)),
            whole((3, SLOTS, CONV)),
            by_slot((2, CONV)),
            by_slot((2, INNER)),
            by_slot((2, HEADS)),
            whole((1, HEADS)),
            whole((1, HEADS)),
            whole((1, HEADS)),
            whole((4, CONV)),
            whole((1, INNER)),
        ],
        out_specs=(by_slot((2, INNER)), whole((16, CONV))),
        compiler_params=params(),
        cost_estimate=cost(8),
    )(move_src, state, tail, fresh, gate, dt_raw, a_log, dt_bias, skip, conv_w, gain)


def landed_kernel(
    move_src,
    move_dst,
    shares,
    kept_h,
    mixed,
    attended,
    out,
    attn_out,
    final,
    arrived,
    src_s,
    dst_s,
    final_v,
    pages,
    mixed_row,
    attn_row,
    kept,
    sems,
):
    scalars = [
        pltpu.make_async_copy(move_src, src_s, sems.at[7]),
        pltpu.make_async_copy(move_dst, dst_s, sems.at[8]),
        pltpu.make_async_copy(kept_h, kept, sems.at[9]),
    ]
    for copy in scalars:
        copy.start()
    for kv in range(2 * PPR):
        for head in range(TP):
            at = PAGE_AT + TOK * (head % 2)
            pages[kv // 2, kv % 2, :, head * 128 : head * 128 + 128] = shares[
                kv * 4 + head // 2, at : at + TOK, :
            ]
    sent = [pltpu.make_async_copy(pages, arrived, sems.at[0])]
    sent[0].start()
    for copy in scalars[:2]:
        copy.wait()
    here = src_s[lax.axis_index("inst")]
    land = here & (SLOTS - 1)
    origin = jnp.int32(0)
    for j in range(N_INST):
        origin = jnp.where(dst_s[j] == here, j, origin)
    pieces = [
        shares[(origin + 1 + r) & (N_INST - 1), HEAD_AT:ROWS_2, :].astype(F32)
        for r in range(TAIL_ROWS // 2)
    ]
    tail = jnp.concatenate(
        [
            jnp.concatenate(
                [pieces[row // 2][row % 2 : row % 2 + 1, :] for row in range(tap * 20, tap * 20 + 20)], 1
            )
            for tap in range(3)
        ],
        0,
    )
    left = shares[:, 0:64, :].reshape(INNER, 128)
    right = shares[:, 64:128, :].reshape(INNER, 128)
    scalars[2].wait()
    conv = convolve(tail, kept[0:2, :], kept[2:6, :])
    scales = [kept[6 + k : 7 + k, 0:INNER] for k in range(5)]
    step1, step2, keep1, keep2, _ = scales
    a1 = keep2 * step1 * conv[0:1, :INNER]
    a2 = step2 * conv[1:2, :INNER]
    b1 = conv[0:1, INNER : INNER + STATE_N]
    b2 = conv[1:2, INNER : INNER + STATE_N]
    keep = keep1 * keep2
    zeros = jnp.zeros((7, INNER), F32)

    def again(value):
        high = value.astype(BF).astype(F32)
        rest = value - high
        middle = rest.astype(BF).astype(F32)
        return high, middle, rest - middle

    kh, km, kl = again(keep)
    a1h, a1l, _ = again(a1)
    a2h, a2l, _ = again(a2)
    rows = jnp.concatenate([kh, km, kl, a1h, a1l, a1h, a2h, a2l, a2h, zeros], 0)
    columns = rows.T.astype(BF)
    b1h, b1l, _ = again(b1)
    b2h, b2l, _ = again(b2)
    none = jnp.zeros((3, STATE_N), F32)
    inner = jnp.concatenate(
        [none, b1h, b1h, b1l, b2h, b2h, b2l, jnp.zeros((7, STATE_N), F32)], 0
    ).astype(BF)
    row = lax.broadcasted_iota(jnp.int32, (16, 128), 0)
    ones = jnp.where(row < 3, 1.0, 0.0).astype(BF)
    heads = 8
    block = heads * HEAD_P
    for part in range(HEADS // heads):
        at = part * block
        some = columns[at : at + block]
        share = dot_nn(some, ones)
        for half, source in enumerate((left, right)):
            added = dot_nn(some, inner[:, half * 128 : half * 128 + 128])
            result = source[at : at + block].astype(F32) * share + added
            final_v[part * heads : part * heads + heads, :, half * 128 : half * 128 + 128] = result.astype(
                BF
            ).reshape(heads, HEAD_P, 128)
        copy = pltpu.make_async_copy(
            final_v.at[pl.ds(part * heads, heads)],
            final.at[0, pl.ds(part * heads, heads)],
            sems.at[1 + part],
        )
        copy.start()
        sent.append(copy)
    rows = shares[origin, HEAD_AT:ROWS_2, :].astype(F32)
    attn_row[...] = jnp.concatenate([rows[2 * h : 2 * h + 2] for h in range(8)], 1).astype(BF)
    sent.append(pltpu.make_async_copy(attn_row, attn_out.at[land], sems.at[5]))
    sent[-1].start()
    mixed_row[...] = mixer(
        lambda lhs: dot_nt(lhs[:, :128], left) + dot_nt(lhs[:, 128:], right),
        conv,
        scales,
        kept[11:13, 0:INNER],
        kept[13:14, 0:INNER],
    )
    sent.append(pltpu.make_async_copy(mixed_row, out.at[land], sems.at[6]))
    sent[-1].start()
    for copy in sent:
        copy.wait()


def landed(move_src, move_dst, shares, kept, mixed, attended):
    return pl.pallas_call(
        landed_kernel,
        out_shape=(
            jax.ShapeDtypeStruct(mixed.shape, BF),
            jax.ShapeDtypeStruct(attended.shape, BF),
            jax.ShapeDtypeStruct((1, HEADS, HEAD_P, STATE_N), BF),
            jax.ShapeDtypeStruct((PPR, 2, TOK, TP * 128), BF),
        ),
        in_specs=[ANY, ANY, VMEM, ANY, ANY, ANY],
        out_specs=(ANY,) * 4,
        input_output_aliases={4: 0, 5: 1},
        scratch_shapes=[
            pltpu.SMEM(move_src.shape, jnp.int32),
            pltpu.SMEM(move_dst.shape, jnp.int32),
            pltpu.VMEM((HEADS, HEAD_P, STATE_N), BF),
            pltpu.VMEM((PPR, 2, TOK, TP * 128), BF),
            pltpu.VMEM(mixed.shape[1:], BF),
            pltpu.VMEM(attended.shape[1:], BF),
            pltpu.VMEM(kept.shape, F32),
            pltpu.SemaphoreType.DMA((10,)),
        ],
        compiler_params=params(),
        cost_estimate=cost(4),
    )(in_hbm(move_src), in_hbm(move_dst), shares, in_hbm(kept), in_hbm(mixed), in_hbm(attended))


def attend(q_rows, keys, values, new_keys, new_values, length, flip):
    pad = jnp.zeros((TOK - 2, 128), F32)
    new_keys = jnp.concatenate([new_keys, pad], 0).astype(BF)
    new_values = jnp.concatenate([new_values, pad], 0).astype(BF)
    cached = PPR * TP * TOK
    all_keys = jnp.concatenate(keys + [new_keys], 0)
    all_values = jnp.concatenate(values + [new_values], 0)
    scores = dot_nt(q_rows, all_keys) * (HEAD_D**-0.5)
    shape = (16, cached + TOK)
    column = lax.broadcasted_iota(jnp.int32, shape, 1)
    step = lax.broadcasted_iota(jnp.int32, shape, 0) & 1
    held = (column >> 4) & (TP - 1)
    position = (column & ~127) + ((held ^ flip) << 4) + (column & 15)
    allowed = jnp.where(column < cached, position - length, column - cached - step - 1) < 0
    peak = jnp.max(jnp.where(allowed, scores, -1e30), -1, keepdims=True)
    weights = jnp.where(allowed, jnp.exp(scores - peak), 0.0)
    total = jnp.sum(weights, -1, keepdims=True)
    high, low = halves(weights)
    return (dot_nn(high, all_values) + dot_nn(low, all_values)) / total


def attend_all_kernel(table, lengths, queries, new_kv, *refs):
    pairs, out = refs[: TP // 2], refs[TP // 2]
    inst, me = lax.axis_index("inst"), lax.axis_index("tp")

    def one(slot, carry):
        keys, values = [], []
        for page in range(PPR):
            at = table[page, slot]
            for d in range(TP):
                keys.append(pairs[d // 2][d % 2, 2 * at])
                values.append(pairs[d // 2][d % 2, 2 * at + 1])
        length = lengths[inst * SLOTS + slot]
        q_rows = head_rows(queries[slot].astype(F32)).astype(BF)
        fresh = new_kv[slot].astype(F32)
        rows = attend(q_rows, keys, values, fresh[:, 0], fresh[:, 1], length, me)
        out[slot] = jnp.concatenate([rows[2 * h : 2 * h + 2] for h in range(8)], 1).astype(BF)
        return carry

    lax.fori_loop(0, SLOTS, one, 0)


def attend_all(table, lengths, queries, new_kv, pairs):
    return pl.pallas_call(
        attend_all_kernel,
        out_shape=jax.ShapeDtypeStruct(queries.shape, BF),
        in_specs=[SMEM, SMEM] + [VMEM] * (2 + TP // 2),
        out_specs=VMEM,
        compiler_params=params(),
        cost_estimate=cost(4),
    )(table, lengths, queries, new_kv, *pairs)


def shards(
    ssm_state,
    conv_tail,
    kv_pool,
    page_table,
    lengths,
    move_src,
    move_dst,
    x_in,
    z_gate,
    dt_raw,
    queries,
    new_kv,
    a_log,
    dt_bias,
    skip_d,
    conv_w,
    norm_gain,
):
    tail = jnp.transpose(conv_tail, (1, 0, 2))
    table = jnp.transpose(page_table, (1, 0))
    a_row, bias_row, skip_row = a_log[None], dt_bias[None], skip_d[None]
    gain_row = norm_gain[None]
    small = (x_in, z_gate, dt_raw, a_row, bias_row, skip_row, conv_w, gain_row)

    packed = pack(move_src, table, ssm_state, tail, kv_pool, queries, new_kv)
    spread = lax.all_to_all(packed, "inst", 0, 0, tiled=True)

    pool = kv_pool.reshape((-1,) + kv_pool.shape[2:])
    pairs = exchange(*split_heads(pool))
    mixed, kept = mixer_all(move_src, ssm_state, tail, *small)
    keys, values = gather(move_src, table, pairs)
    spread, mixed, kept, pairs, keys, values = lax.optimization_barrier(
        (spread, mixed, kept, pairs, keys, values)
    )

    turned = turn(move_src, move_dst, lengths, spread, keys, values)
    turned, pairs = lax.optimization_barrier((turned, pairs))
    shares = lax.all_to_all(turned, "inst", 0, 0, tiled=True)

    attended = attend_all(table, lengths, queries, new_kv, pairs)
    mamba_out, attn_out, arrived_state, arrived_pages = landed(
        move_src, move_dst, shares, kept, mixed, attended
    )
    return mamba_out, attn_out, arrived_state, arrived_pages


def solution(mesh):
    in_specs = (
        P("inst", "tp", None, None),
        P("inst", None, "tp"),
        P("inst", None, "tp", None),
        P("inst", None),
        P(),
        P(),
        P(),
        P("inst", None, "tp"),
        P("inst", None, "tp"),
        P("inst", None, "tp"),
        P("inst", None, "tp"),
        P("inst", None, None, "tp"),
        P("tp"),
        P("tp"),
        P("tp"),
        P(None, "tp"),
        P("tp"),
    )
    out_specs = (
        P("inst", None, "tp"),
        P("inst", None, "tp"),
        P("inst", "tp", None, None),
        P("inst", None, "tp", None),
    )
    return jax.shard_map(shards, mesh=mesh, in_specs=in_specs, out_specs=out_specs, check_vma=False)
```

```python
import functools

import jax
import jax.numpy as jnp
from jax import lax
from jax.experimental import pallas as pl
from jax.experimental.pallas import tpu as pltpu
from jax.sharding import PartitionSpec as P

BF = jnp.bfloat16
F32 = jnp.float32
HEADS = 32
HEAD_P = 64
INNER = 2048
STATE_N = 256
CONV = 2560
HEAD_D = 128
PAGE = 128
PPR = 4
TP = 8
TOK = 16
N_INST = 32
SLOTS = 8
PAGE_AT = 4096
TAIL_AT = 5120
TAIL_ROWS = 60
SHARES = N_INST - 2
ROWS = 176
ALL_ROWS = SHARES * ROWS

SMEM = pl.BlockSpec(memory_space=pltpu.SMEM)
VMEM = pl.BlockSpec(memory_space=pltpu.VMEM)
ANY = pl.BlockSpec(memory_space=pl.ANY)
HBM = pl.BlockSpec(memory_space=pltpu.HBM)


def params():
    return pltpu.CompilerParams(vmem_limit_bytes=48 * 1024 * 1024)


def cost(microseconds):
    return pl.CostEstimate(
        flops=int(microseconds * 5e8), bytes_accessed=int(microseconds * 3e6), transcendentals=0
    )


def in_hbm(value):
    return pltpu.with_memory_space_constraint(value, pltpu.HBM)


def sender_to(move_dst, inst):
    found = jnp.int32(0)
    for j in range(N_INST):
        found = jnp.where((move_dst[j] >> 3) == inst, j, found)
    return found


def holder(share, inst, source):
    low = jnp.minimum(inst, source)
    high = jnp.where(inst == source, 2 * N_INST, jnp.maximum(inst, source))
    place = jnp.where(share >= low, share + 1, share)
    return jnp.where(place >= high, place + 1, place)


def halves(value):
    high = value.astype(BF)
    low = (value - high.astype(F32)).astype(BF)
    return high, low


def thirds(value):
    high = value.astype(BF)
    rest = value - high.astype(F32)
    middle = rest.astype(BF)
    low = (rest - middle.astype(F32)).astype(BF)
    return high, middle, low


def dot_nt(left, right):
    return lax.dot_general(left, right, (((1,), (1,)), ((), ())), preferred_element_type=F32)


def dot_nn(left, right):
    return lax.dot_general(left, right, (((1,), (0,)), ((), ())), preferred_element_type=F32)


def head_rows(value):
    return jnp.concatenate([value[:, h * 128 : h * 128 + 128] for h in range(8)], 0)


def pack_kernel(
    move_src,
    move_dst,
    table,
    state,
    tail,
    pool,
    queries,
    new_kv,
    packed,
    src_s,
    dst_s,
    table_s,
    tail_v,
    queries_v,
    new_v,
    pages,
    tail_rows,
    asked,
    state_v,
    rows_v,
    sems,
    page_sems,
    state_sems,
    out_sems,
):
    early = [
        pltpu.make_async_copy(move_src, src_s, sems.at[0]),
        pltpu.make_async_copy(table, table_s, sems.at[1]),
        pltpu.make_async_copy(move_dst, dst_s, sems.at[2]),
        pltpu.make_async_copy(tail, tail_v, sems.at[3]),
        pltpu.make_async_copy(queries, queries_v, sems.at[4]),
        pltpu.make_async_copy(new_kv, new_v, sems.at[5]),
    ]
    for copy in early:
        copy.start()
    early[0].wait()
    inst = lax.axis_index("inst")
    leave = src_s[inst] & (SLOTS - 1)
    parts = 4
    heads = HEADS // parts
    states = [
        pltpu.make_async_copy(
            state.at[leave, pl.ds(part * heads, heads)],
            state_v.at[pl.ds(part * heads, heads)],
            state_sems.at[part],
        )
        for part in range(parts)
    ]
    for copy in states:
        copy.start()
    early[1].wait()
    page_copies = [
        pltpu.make_async_copy(pool.at[table_s[page, leave]], pages.at[page], page_sems.at[page])
        for page in range(PPR)
    ]
    for copy in page_copies:
        copy.start()
    for copy in early[2:]:
        copy.wait()
    source = sender_to(dst_s, inst)
    fresh = new_v[leave].astype(F32)
    asked[...] = jnp.concatenate(
        [head_rows(queries_v[leave].astype(F32)), fresh[0], fresh[1], jnp.zeros((12, 128), F32)], 0
    ).astype(BF)
    sent = [pltpu.make_async_copy(asked, packed.at[source, pl.ds(0, 32), :], out_sems.at[SHARES])]
    sent[0].start()
    slot = lax.broadcasted_iota(jnp.int32, (3, SLOTS, CONV), 1)
    mine = jnp.sum(jnp.where(slot == leave, tail_v[...].astype(F32), 0.0), 1)
    tail_rows[...] = jnp.zeros_like(tail_rows)
    for row in range(TAIL_ROWS):
        tap, at = row // 20, (row % 20) * 128
        tail_rows[row : row + 1, :] = mine[tap : tap + 1, at : at + 128]
    rows_v[TAIL_AT:ALL_ROWS, :] = tail_rows[...].astype(BF)
    for copy in page_copies:
        copy.wait()
    for kv in range(2 * PPR):
        for head in range(TP):
            at = PAGE_AT + TOK * (kv * TP + head)
            rows_v[at : at + TOK, :] = pages[kv // 2, kv % 2, :, head * 128 : head * 128 + 128]
    for part in range(parts):
        states[part].wait()
        for head in range(part * heads, part * heads + heads):
            for half in range(2):
                at = head * 128 + half * 64
                rows_v[at : at + 64, :] = state_v[head, :, half * 128 : half * 128 + 128]
        ready = SHARES if part == parts - 1 else (part + 1) * heads * 128 // ROWS
        for share in range(len(sent) - 1, ready):
            copy = pltpu.make_async_copy(
                rows_v.at[pl.ds(share * ROWS, ROWS), :],
                packed.at[holder(share, inst, source)],
                out_sems.at[share],
            )
            copy.start()
            sent.append(copy)
    for copy in sent:
        copy.wait()


def pack(move_src, move_dst, table, state, tail, pool, queries, new_kv):
    return pl.pallas_call(
        pack_kernel,
        out_shape=jax.ShapeDtypeStruct((N_INST, ROWS, 128), BF),
        in_specs=[ANY] * 8,
        out_specs=HBM,
        scratch_shapes=[
            pltpu.SMEM(move_src.shape, jnp.int32),
            pltpu.SMEM(move_dst.shape, jnp.int32),
            pltpu.SMEM(table.shape, jnp.int32),
            pltpu.VMEM(tail.shape, BF),
            pltpu.VMEM(queries.shape, BF),
            pltpu.VMEM(new_kv.shape, BF),
            pltpu.VMEM((PPR, 2, TOK, TP * 128), BF),
            pltpu.VMEM((ALL_ROWS - TAIL_AT, 128), F32),
            pltpu.VMEM((32, 128), BF),
            pltpu.VMEM(state.shape[1:], BF),
            pltpu.VMEM((ALL_ROWS, 128), BF),
            pltpu.SemaphoreType.DMA((6,)),
            pltpu.SemaphoreType.DMA((PPR,)),
            pltpu.SemaphoreType.DMA((4,)),
            pltpu.SemaphoreType.DMA((SHARES + 1,)),
        ],
        cost_estimate=cost(3),
    )(move_src, move_dst, table, state, tail, pool, queries, new_kv)


def turn_kernel(move_src, move_dst, table, lengths, shares, *refs):
    pairs, (out, rows, held, slab_sems, held_sems, row_sem) = refs[: TP // 2], refs[TP // 2 :]
    inst, me = lax.axis_index("inst"), lax.axis_index("tp")
    leave = move_src[inst] & (SLOTS - 1)
    cached = []
    for page in range(PPR):
        at = 2 * table[page, leave]
        for e in range(TP // 2):
            cached.append(
                pltpu.make_async_copy(
                    pairs[e].at[:, pl.ds(at, 2)], held.at[page, e], held_sems.at[page * (TP // 2) + e]
                )
            )
    for copy in cached:
        copy.start()
    slabs = [
        pltpu.make_async_copy(shares.at[j], out.at[move_dst[j] >> 3], slab_sems.at[j])
        for j in range(N_INST)
    ]
    for j, slab in enumerate(slabs):
        pl.when(inst != j)(slab.start)
    target = move_dst[inst] >> 3
    fresh = shares[target, 16:32, :].astype(F32)
    new_keys = jnp.concatenate([fresh[0:1], fresh[2:3]], 0)
    new_values = jnp.concatenate([fresh[1:2], fresh[3:4]], 0)
    length = lengths[move_src[inst]]
    for copy in cached:
        copy.wait()
    keys = [held[p, d // 2, d % 2, 0] for p in range(PPR) for d in range(TP)]
    values = [held[p, d // 2, d % 2, 1] for p in range(PPR) for d in range(TP)]
    result = attend(shares[target, 0:16, :], keys, values, new_keys, new_values, length, me)
    rows[...] = result.astype(BF)
    last = pltpu.make_async_copy(rows, out.at[target, pl.ds(0, 16), :], row_sem.at[0])
    last.start()
    for j, slab in enumerate(slabs):
        pl.when(inst != j)(slab.wait)
    last.wait()


def turn(move_src, move_dst, table, lengths, shares, pairs):
    return pl.pallas_call(
        turn_kernel,
        out_shape=jax.ShapeDtypeStruct(shares.shape, BF),
        in_specs=[SMEM] * 4 + [VMEM] + [ANY] * (TP // 2),
        out_specs=HBM,
        scratch_shapes=[
            pltpu.VMEM((16, 128), BF),
            pltpu.VMEM((PPR, TP // 2, 2, 2, TOK, 128), BF),
            pltpu.SemaphoreType.DMA((N_INST,)),
            pltpu.SemaphoreType.DMA((PPR * TP // 2,)),
            pltpu.SemaphoreType.DMA((1,)),
        ],
        compiler_params=params(),
        cost_estimate=cost(3),
    )(move_src, move_dst, table, lengths, in_hbm(shares), *pairs)


def split_heads_kernel(pool, own, other, sems):
    me = lax.axis_index("tp")
    copies = []
    for e in range(TP // 2):
        for b, ref in enumerate((own, other)):
            at = pl.multiple_of((me ^ (2 * e + b)) * 128, 128)
            copies.append(
                pltpu.make_async_copy(pool.at[:, :, pl.ds(at, 128)], ref.at[e], sems.at[2 * e + b])
            )
    for copy in copies:
        copy.start()
    for copy in copies:
        copy.wait()


def split_heads(pool):
    part = jax.ShapeDtypeStruct((TP // 2,) + pool.shape[:2] + (128,), BF)
    return pl.pallas_call(
        split_heads_kernel,
        out_shape=(part, part),
        in_specs=[ANY],
        out_specs=(ANY, ANY),
        scratch_shapes=[pltpu.SemaphoreType.DMA((TP,))],
        compiler_params=params(),
        cost_estimate=cost(2),
    )(pool)


def pair_kernel(own, other, *refs):
    outs, sems = refs[: TP // 2], refs[TP // 2]
    copies = []
    for e in range(TP // 2):
        for b, ref in enumerate((own, other)):
            copies.append(pltpu.make_async_copy(ref.at[e], outs[e].at[b], sems.at[2 * e + b]))
    for copy in copies:
        copy.start()
    for copy in copies:
        copy.wait()


def exchange(own, other):
    swapped = lax.ppermute(other, "tp", [(i, i ^ 1) for i in range(TP)])
    pair = jax.ShapeDtypeStruct((2,) + own.shape[1:], BF)
    pairs = pl.pallas_call(
        pair_kernel,
        out_shape=(pair,) * (TP // 2),
        in_specs=[ANY, ANY],
        out_specs=(ANY,) * (TP // 2),
        scratch_shapes=[pltpu.SemaphoreType.DMA((TP,))],
        compiler_params=params(),
        cost_estimate=cost(1),
    )(own, swapped)
    return [pairs[0]] + [
        lax.ppermute(pairs[e], "tp", [(i, i ^ (2 * e)) for i in range(TP)]) for e in range(1, TP // 2)
    ]


def silu(value):
    return value * (1.0 / (1.0 + jnp.exp(-value)))


def convolve(tail, fresh, conv_w):
    window = [tail[k : k + 1] for k in range(3)] + [fresh[k : k + 1] for k in range(2)]
    steps = []
    for t in range(2):
        total = conv_w[0:1] * window[t]
        for k in range(1, 4):
            total = total + conv_w[k : k + 1] * window[t + k]
        steps.append(total)
    return silu(jnp.concatenate(steps, 0))


def per_channel(dt_raw, a_log, dt_bias, skip):
    raw = dt_raw + dt_bias
    step = jnp.maximum(raw, 0.0) + jnp.log1p(jnp.exp(-jnp.abs(raw)))
    retain = jnp.exp(-step * jnp.exp(a_log))
    per_head = jnp.concatenate([step, retain, skip, jnp.zeros((3, HEADS), F32)], 0)
    head_row = lax.broadcasted_iota(jnp.int32, (HEADS, INNER), 0)
    channel = lax.broadcasted_iota(jnp.int32, (HEADS, INNER), 1)
    spread = jnp.where(channel // HEAD_P == head_row, 1.0, 0.0).astype(BF)
    rows = sum(dot_nn(part, spread) for part in thirds(per_head))
    return [rows[k : k + 1] for k in range(5)]


def mixer(state_dots, conv, scales, gate, gain):
    b_in = conv[:, INNER : INNER + STATE_N]
    c_out = conv[:, INNER + STATE_N :]
    step1, step2, keep1, keep2, skip_c = scales
    c_high, c_low = halves(c_out)
    dots = state_dots(jnp.concatenate([c_high, c_low, jnp.zeros((12, STATE_N), BF)], 0))
    dots = dots[0:2] + dots[2:4]
    b1, b2, c1, c2 = b_in[0:1], b_in[1:2], c_out[0:1], c_out[1:2]
    x1, x2 = conv[0:1, :INNER], conv[1:2, :INNER]
    u1, u2 = step1 * x1, step2 * x2
    bc11 = jnp.sum(b1 * c1, -1, keepdims=True)
    bc12 = jnp.sum(b1 * c2, -1, keepdims=True)
    bc22 = jnp.sum(b2 * c2, -1, keepdims=True)
    y1 = keep1 * dots[0:1] + u1 * bc11 + skip_c * x1
    y2 = keep2 * (keep1 * dots[1:2] + u1 * bc12) + u2 * bc22 + skip_c * x2
    y = jnp.concatenate([y1, y2], 0) * gate
    y = y * lax.rsqrt(jnp.mean(y * y, -1, keepdims=True) + 1e-05) * gain
    return y.astype(BF)


def mixer_all_kernel(
    move_src, state, tail, fresh, gate, dt_raw, a_log, dt_bias, skip, conv_w, gain, out, kept
):
    here = pl.program_id(0)
    slot = lax.broadcasted_iota(jnp.int32, (3, SLOTS, CONV), 1)
    mine = jnp.sum(jnp.where(slot == here, tail[...].astype(F32), 0.0), 1)
    rows = state[0].reshape(INNER, STATE_N)
    new = fresh[0].astype(F32)
    scales = per_channel(dt_raw[0], a_log[...], dt_bias[...], skip[...])
    gated = silu(gate[0].astype(F32))
    out[0] = mixer(
        lambda lhs: dot_nt(lhs, rows), convolve(mine, new, conv_w[...]), scales, gated, gain[...]
    )

    @pl.when(here == (move_src[lax.axis_index("inst")] & (SLOTS - 1)))
    def _():
        kept[0:2, :] = new
        kept[2:6, :] = conv_w[...]
        for k in range(5):
            kept[6 + k : 7 + k, 0:INNER] = scales[k]
        kept[11:13, 0:INNER] = gated
        kept[13:14, 0:INNER] = gain[...]


def mixer_all(move_src, state, tail, fresh, gate, dt_raw, a_log, dt_bias, skip, conv_w, gain):
    def whole(shape):
        return pl.BlockSpec(shape, lambda s: (0,) * len(shape))

    def by_slot(shape):
        return pl.BlockSpec((1,) + shape, lambda s: (s,) + (0,) * len(shape))

    return pl.pallas_call(
        mixer_all_kernel,
        grid=(SLOTS,),
        out_shape=(
            jax.ShapeDtypeStruct((SLOTS, 2, INNER), BF),
            jax.ShapeDtypeStruct((16, CONV), F32),
        ),
        in_specs=[
            SMEM,
            by_slot((HEADS, HEAD_P, STATE_N)),
            whole((3, SLOTS, CONV)),
            by_slot((2, CONV)),
            by_slot((2, INNER)),
            by_slot((2, HEADS)),
            whole((1, HEADS)),
            whole((1, HEADS)),
            whole((1, HEADS)),
            whole((4, CONV)),
            whole((1, INNER)),
        ],
        out_specs=(by_slot((2, INNER)), whole((16, CONV))),
        compiler_params=params(),
        cost_estimate=cost(8),
    )(move_src, state, tail, fresh, gate, dt_raw, a_log, dt_bias, skip, conv_w, gain)


def landed_kernel(
    move_src,
    move_dst,
    shares,
    kept_h,
    mixed,
    attended,
    out,
    attn_out,
    final,
    arrived,
    src_s,
    dst_s,
    final_v,
    pages,
    mixed_row,
    attn_row,
    kept,
    rows_v,
    sems,
):
    scalars = [
        pltpu.make_async_copy(move_src, src_s, sems.at[7]),
        pltpu.make_async_copy(move_dst, dst_s, sems.at[8]),
        pltpu.make_async_copy(kept_h, kept, sems.at[9]),
    ]
    for copy in scalars:
        copy.start()
    for copy in scalars[:2]:
        copy.wait()
    inst = lax.axis_index("inst")
    land = src_s[inst] & (SLOTS - 1)
    origin = sender_to(dst_s, inst)
    source = sender_to(dst_s, origin)
    for share in reversed(range(SHARES)):
        rows_v[share * ROWS : share * ROWS + ROWS, :] = shares[holder(share, origin, source)]
    for kv in range(2 * PPR):
        for head in range(TP):
            at = PAGE_AT + TOK * (kv * TP + head)
            pages[kv // 2, kv % 2, :, head * 128 : head * 128 + 128] = rows_v[at : at + TOK, :]
    sent = [pltpu.make_async_copy(pages, arrived, sems.at[0])]
    sent[0].start()
    pieces = rows_v[TAIL_AT : TAIL_AT + 64, :].astype(F32)
    tail = jnp.concatenate(
        [
            jnp.concatenate([pieces[row : row + 1] for row in range(tap * 20, tap * 20 + 20)], 1)
            for tap in range(3)
        ],
        0,
    )
    state = rows_v[0:PAGE_AT, :].reshape(HEADS, 128, 128)
    left = state[:, 0:64, :].reshape(INNER, 128)
    right = state[:, 64:128, :].reshape(INNER, 128)
    scalars[2].wait()
    conv = convolve(tail, kept[0:2, :], kept[2:6, :])
    scales = [kept[6 + k : 7 + k, 0:INNER] for k in range(5)]
    step1, step2, keep1, keep2, _ = scales
    a1 = keep2 * step1 * conv[0:1, :INNER]
    a2 = step2 * conv[1:2, :INNER]
    b1 = conv[0:1, INNER : INNER + STATE_N]
    b2 = conv[1:2, INNER : INNER + STATE_N]
    keep = keep1 * keep2
    zeros = jnp.zeros((7, INNER), F32)

    def again(value):
        high = value.astype(BF).astype(F32)
        rest = value - high
        middle = rest.astype(BF).astype(F32)
        return high, middle, rest - middle

    kh, km, kl = again(keep)
    a1h, a1l, _ = again(a1)
    a2h, a2l, _ = again(a2)
    rows = jnp.concatenate([kh, km, kl, a1h, a1l, a1h, a2h, a2l, a2h, zeros], 0)
    columns = rows.T.astype(BF)
    b1h, b1l, _ = again(b1)
    b2h, b2l, _ = again(b2)
    none = jnp.zeros((3, STATE_N), F32)
    inner = jnp.concatenate(
        [none, b1h, b1h, b1l, b2h, b2h, b2l, jnp.zeros((7, STATE_N), F32)], 0
    ).astype(BF)
    row = lax.broadcasted_iota(jnp.int32, (16, 128), 0)
    ones = jnp.where(row < 3, 1.0, 0.0).astype(BF)
    heads = 8
    block = heads * HEAD_P
    for part in range(HEADS // heads):
        at = part * block
        some = columns[at : at + block]
        share = dot_nn(some, ones)
        for half, source in enumerate((left, right)):
            added = dot_nn(some, inner[:, half * 128 : half * 128 + 128])
            result = source[at : at + block].astype(F32) * share + added
            final_v[part * heads : part * heads + heads, :, half * 128 : half * 128 + 128] = result.astype(
                BF
            ).reshape(heads, HEAD_P, 128)
        copy = pltpu.make_async_copy(
            final_v.at[pl.ds(part * heads, heads)],
            final.at[0, pl.ds(part * heads, heads)],
            sems.at[1 + part],
        )
        copy.start()
        sent.append(copy)
    rows = shares[origin, 0:16, :].astype(F32)
    attn_row[...] = jnp.concatenate([rows[2 * h : 2 * h + 2] for h in range(8)], 1).astype(BF)
    sent.append(pltpu.make_async_copy(attn_row, attn_out.at[land], sems.at[5]))
    sent[-1].start()
    mixed_row[...] = mixer(
        lambda lhs: dot_nt(lhs[:, :128], left) + dot_nt(lhs[:, 128:], right),
        conv,
        scales,
        kept[11:13, 0:INNER],
        kept[13:14, 0:INNER],
    )
    sent.append(pltpu.make_async_copy(mixed_row, out.at[land], sems.at[6]))
    sent[-1].start()
    for copy in sent:
        copy.wait()


def landed(move_src, move_dst, shares, kept, mixed, attended):
    return pl.pallas_call(
        landed_kernel,
        out_shape=(
            jax.ShapeDtypeStruct(mixed.shape, BF),
            jax.ShapeDtypeStruct(attended.shape, BF),
            jax.ShapeDtypeStruct((1, HEADS, HEAD_P, STATE_N), BF),
            jax.ShapeDtypeStruct((PPR, 2, TOK, TP * 128), BF),
        ),
        in_specs=[ANY, ANY, VMEM, ANY, ANY, ANY],
        out_specs=(ANY,) * 4,
        input_output_aliases={4: 0, 5: 1},
        scratch_shapes=[
            pltpu.SMEM(move_src.shape, jnp.int32),
            pltpu.SMEM(move_dst.shape, jnp.int32),
            pltpu.VMEM((HEADS, HEAD_P, STATE_N), BF),
            pltpu.VMEM((PPR, 2, TOK, TP * 128), BF),
            pltpu.VMEM(mixed.shape[1:], BF),
            pltpu.VMEM(attended.shape[1:], BF),
            pltpu.VMEM(kept.shape, F32),
            pltpu.VMEM((ALL_ROWS, 128), BF),
            pltpu.SemaphoreType.DMA((10,)),
        ],
        compiler_params=params(),
        cost_estimate=cost(4),
    )(in_hbm(move_src), in_hbm(move_dst), shares, in_hbm(kept), in_hbm(mixed), in_hbm(attended))


def attend(q_rows, keys, values, new_keys, new_values, length, flip):
    pad = jnp.zeros((TOK - 2, 128), F32)
    new_keys = jnp.concatenate([new_keys, pad], 0).astype(BF)
    new_values = jnp.concatenate([new_values, pad], 0).astype(BF)
    cached = PPR * TP * TOK
    all_keys = jnp.concatenate(keys + [new_keys], 0)
    all_values = jnp.concatenate(values + [new_values], 0)
    scores = dot_nt(q_rows, all_keys) * (HEAD_D**-0.5)
    shape = (16, cached + TOK)
    column = lax.broadcasted_iota(jnp.int32, shape, 1)
    step = lax.broadcasted_iota(jnp.int32, shape, 0) & 1
    held = (column >> 4) & (TP - 1)
    position = (column & ~127) + ((held ^ flip) << 4) + (column & 15)
    allowed = jnp.where(column < cached, position - length, column - cached - step - 1) < 0
    peak = jnp.max(jnp.where(allowed, scores, -1e30), -1, keepdims=True)
    weights = jnp.where(allowed, jnp.exp(scores - peak), 0.0)
    total = jnp.sum(weights, -1, keepdims=True)
    high, low = halves(weights)
    return (dot_nn(high, all_values) + dot_nn(low, all_values)) / total


def attend_all_kernel(table, lengths, queries, new_kv, *refs):
    pairs, out = refs[: TP // 2], refs[TP // 2]
    inst, me = lax.axis_index("inst"), lax.axis_index("tp")

    def one(slot, carry):
        keys, values = [], []
        for page in range(PPR):
            at = table[page, slot]
            for d in range(TP):
                keys.append(pairs[d // 2][d % 2, 2 * at])
                values.append(pairs[d // 2][d % 2, 2 * at + 1])
        length = lengths[inst * SLOTS + slot]
        q_rows = head_rows(queries[slot].astype(F32)).astype(BF)
        fresh = new_kv[slot].astype(F32)
        rows = attend(q_rows, keys, values, fresh[:, 0], fresh[:, 1], length, me)
        out[slot] = jnp.concatenate([rows[2 * h : 2 * h + 2] for h in range(8)], 1).astype(BF)
        return carry

    lax.fori_loop(0, SLOTS, one, 0)


def attend_all(table, lengths, queries, new_kv, pairs):
    return pl.pallas_call(
        attend_all_kernel,
        out_shape=jax.ShapeDtypeStruct(queries.shape, BF),
        in_specs=[SMEM, SMEM] + [VMEM] * (2 + TP // 2),
        out_specs=VMEM,
        compiler_params=params(),
        cost_estimate=cost(4),
    )(table, lengths, queries, new_kv, *pairs)


def shards(
    ssm_state,
    conv_tail,
    kv_pool,
    page_table,
    lengths,
    move_src,
    move_dst,
    x_in,
    z_gate,
    dt_raw,
    queries,
    new_kv,
    a_log,
    dt_bias,
    skip_d,
    conv_w,
    norm_gain,
):
    tail = jnp.transpose(conv_tail, (1, 0, 2))
    table = jnp.transpose(page_table, (1, 0))
    a_row, bias_row, skip_row = a_log[None], dt_bias[None], skip_d[None]
    gain_row = norm_gain[None]
    small = (x_in, z_gate, dt_raw, a_row, bias_row, skip_row, conv_w, gain_row)

    packed = pack(move_src, move_dst, table, ssm_state, tail, kv_pool, queries, new_kv)
    spread = lax.all_to_all(packed, "inst", 0, 0, tiled=True)

    pool = kv_pool.reshape((-1,) + kv_pool.shape[2:])
    pairs = exchange(*split_heads(pool))
    mixed, kept = mixer_all(move_src, ssm_state, tail, *small)
    spread, mixed, kept, pairs = lax.optimization_barrier((spread, mixed, kept, pairs))

    turned = turn(move_src, move_dst, table, lengths, spread, pairs)
    turned, pairs = lax.optimization_barrier((turned, pairs))
    shares = lax.all_to_all(turned, "inst", 0, 0, tiled=True)

    attended = attend_all(table, lengths, queries, new_kv, pairs)
    mamba_out, attn_out, arrived_state, arrived_pages = landed(
        move_src, move_dst, shares, kept, mixed, attended
    )
    return mamba_out, attn_out, arrived_state, arrived_pages


def solution(mesh):
    in_specs = (
        P("inst", "tp", None, None),
        P("inst", None, "tp"),
        P("inst", None, "tp", None),
        P("inst", None),
        P(),
        P(),
        P(),
        P("inst", None, "tp"),
        P("inst", None, "tp"),
        P("inst", None, "tp"),
        P("inst", None, "tp"),
        P("inst", None, None, "tp"),
        P("tp"),
        P("tp"),
        P("tp"),
        P(None, "tp"),
        P("tp"),
    )
    out_specs = (
        P("inst", None, "tp"),
        P("inst", None, "tp"),
        P("inst", "tp", None, None),
        P("inst", None, "tp", None),
    )
    return jax.shard_map(shards, mesh=mesh, in_specs=in_specs, out_specs=out_specs, check_vma=False)
```

```python
import functools

import jax
import jax.numpy as jnp
from jax import lax
from jax.experimental import pallas as pl
from jax.experimental.pallas import tpu as pltpu
from jax.sharding import PartitionSpec as P

BF = jnp.bfloat16
F32 = jnp.float32
HEADS = 32
HEAD_P = 64
INNER = 2048
STATE_N = 256
CONV = 2560
HEAD_D = 128
PAGE = 128
PPR = 4
TP = 8
TOK = 16
N_INST = 32
SLOTS = 8
PAGE_AT = 4096
TAIL_AT = 5120
TAIL_ROWS = 60
SHARES = N_INST - 2
ROWS = 176
ALL_ROWS = SHARES * ROWS

SMEM = pl.BlockSpec(memory_space=pltpu.SMEM)
VMEM = pl.BlockSpec(memory_space=pltpu.VMEM)
ANY = pl.BlockSpec(memory_space=pl.ANY)
HBM = pl.BlockSpec(memory_space=pltpu.HBM)


def params():
    return pltpu.CompilerParams(vmem_limit_bytes=48 * 1024 * 1024)


def cost(microseconds):
    return pl.CostEstimate(
        flops=int(microseconds * 5e8), bytes_accessed=int(microseconds * 3e6), transcendentals=0
    )


def in_hbm(value):
    return pltpu.with_memory_space_constraint(value, pltpu.HBM)


def sender_to(move_dst, inst):
    found = jnp.int32(0)
    for j in range(N_INST):
        found = jnp.where((move_dst[j] >> 3) == inst, j, found)
    return found


def holder(share, inst, source):
    low = jnp.minimum(inst, source)
    high = jnp.where(inst == source, 2 * N_INST, jnp.maximum(inst, source))
    place = jnp.where(share >= low, share + 1, share)
    return jnp.where(place >= high, place + 1, place)


def halves(value):
    high = value.astype(BF)
    low = (value - high.astype(F32)).astype(BF)
    return high, low


def thirds(value):
    high = value.astype(BF)
    rest = value - high.astype(F32)
    middle = rest.astype(BF)
    low = (rest - middle.astype(F32)).astype(BF)
    return high, middle, low


def dot_nt(left, right):
    return lax.dot_general(left, right, (((1,), (1,)), ((), ())), preferred_element_type=F32)


def dot_nn(left, right):
    return lax.dot_general(left, right, (((1,), (0,)), ((), ())), preferred_element_type=F32)


def head_rows(value):
    return jnp.concatenate([value[:, h * 128 : h * 128 + 128] for h in range(8)], 0)


def pack_kernel(
    move_src,
    move_dst,
    table,
    state,
    tail,
    pool,
    queries,
    new_kv,
    packed,
    src_s,
    dst_s,
    table_s,
    tail_v,
    queries_v,
    new_v,
    pages,
    tail_rows,
    asked,
    state_v,
    rows_v,
    sems,
    page_sems,
    state_sems,
    out_sems,
):
    early = [
        pltpu.make_async_copy(move_src, src_s, sems.at[0]),
        pltpu.make_async_copy(table, table_s, sems.at[1]),
        pltpu.make_async_copy(move_dst, dst_s, sems.at[2]),
        pltpu.make_async_copy(tail, tail_v, sems.at[3]),
        pltpu.make_async_copy(queries, queries_v, sems.at[4]),
        pltpu.make_async_copy(new_kv, new_v, sems.at[5]),
    ]
    for copy in early:
        copy.start()
    early[0].wait()
    inst = lax.axis_index("inst")
    leave = src_s[inst] & (SLOTS - 1)
    parts = 4
    heads = HEADS // parts
    states = [
        pltpu.make_async_copy(
            state.at[leave, pl.ds(part * heads, heads)],
            state_v.at[pl.ds(part * heads, heads)],
            state_sems.at[part],
        )
        for part in range(parts)
    ]
    for copy in states:
        copy.start()
    early[1].wait()
    page_copies = [
        pltpu.make_async_copy(pool.at[table_s[page, leave]], pages.at[page], page_sems.at[page])
        for page in range(PPR)
    ]
    for copy in page_copies:
        copy.start()
    for copy in early[2:]:
        copy.wait()
    source = sender_to(dst_s, inst)
    fresh = new_v[leave].astype(F32)
    asked[...] = jnp.concatenate(
        [head_rows(queries_v[leave].astype(F32)), fresh[0], fresh[1], jnp.zeros((12, 128), F32)], 0
    ).astype(BF)
    sent = [pltpu.make_async_copy(asked, packed.at[source, pl.ds(0, 32), :], out_sems.at[SHARES])]
    sent[0].start()
    slot = lax.broadcasted_iota(jnp.int32, (3, SLOTS, CONV), 1)
    mine = jnp.sum(jnp.where(slot == leave, tail_v[...].astype(F32), 0.0), 1)
    tail_rows[...] = jnp.zeros_like(tail_rows)
    for row in range(TAIL_ROWS):
        tap, at = row // 20, (row % 20) * 128
        tail_rows[row : row + 1, :] = mine[tap : tap + 1, at : at + 128]
    rows_v[TAIL_AT:ALL_ROWS, :] = tail_rows[...].astype(BF)
    for copy in page_copies:
        copy.wait()
    for kv in range(2 * PPR):
        for head in range(TP):
            at = PAGE_AT + TOK * (kv * TP + head)
            rows_v[at : at + TOK, :] = pages[kv // 2, kv % 2, :, head * 128 : head * 128 + 128]
    for part in range(parts):
        states[part].wait()
        for head in range(part * heads, part * heads + heads):
            for half in range(2):
                at = head * 128 + half * 64
                rows_v[at : at + 64, :] = state_v[head, :, half * 128 : half * 128 + 128]
        ready = SHARES if part == parts - 1 else (part + 1) * heads * 128 // ROWS
        for share in range(len(sent) - 1, ready):
            copy = pltpu.make_async_copy(
                rows_v.at[pl.ds(share * ROWS, ROWS), :],
                packed.at[holder(share, inst, source)],
                out_sems.at[share],
            )
            copy.start()
            sent.append(copy)
    for copy in sent:
        copy.wait()


def pack(move_src, move_dst, table, state, tail, pool, queries, new_kv):
    return pl.pallas_call(
        pack_kernel,
        out_shape=jax.ShapeDtypeStruct((N_INST, ROWS, 128), BF),
        in_specs=[ANY] * 8,
        out_specs=HBM,
        scratch_shapes=[
            pltpu.SMEM(move_src.shape, jnp.int32),
            pltpu.SMEM(move_dst.shape, jnp.int32),
            pltpu.SMEM(table.shape, jnp.int32),
            pltpu.VMEM(tail.shape, BF),
            pltpu.VMEM(queries.shape, BF),
            pltpu.VMEM(new_kv.shape, BF),
            pltpu.VMEM((PPR, 2, TOK, TP * 128), BF),
            pltpu.VMEM((ALL_ROWS - TAIL_AT, 128), F32),
            pltpu.VMEM((32, 128), BF),
            pltpu.VMEM(state.shape[1:], BF),
            pltpu.VMEM((ALL_ROWS, 128), BF),
            pltpu.SemaphoreType.DMA((6,)),
            pltpu.SemaphoreType.DMA((PPR,)),
            pltpu.SemaphoreType.DMA((4,)),
            pltpu.SemaphoreType.DMA((SHARES + 1,)),
        ],
        cost_estimate=cost(3),
    )(move_src, move_dst, table, state, tail, pool, queries, new_kv)


def turn_kernel(move_src, move_dst, lengths, shares, *refs):
    pairs, (out, rows, slab_sems, row_sem) = refs[: TP // 2], refs[TP // 2 :]
    inst, me = lax.axis_index("inst"), lax.axis_index("tp")
    slabs = [
        pltpu.make_async_copy(shares.at[j], out.at[move_dst[j] >> 3], slab_sems.at[j])
        for j in range(N_INST)
    ]
    for j, slab in enumerate(slabs):
        pl.when(inst != j)(slab.start)
    target = move_dst[inst] >> 3
    fresh = shares[target, 16:32, :].astype(F32)
    new_keys = jnp.concatenate([fresh[0:1], fresh[2:3]], 0)
    new_values = jnp.concatenate([fresh[1:2], fresh[3:4]], 0)
    length = lengths[move_src[inst]]
    keys = [pairs[d // 2][d % 2, 2 * p] for p in range(PPR) for d in range(TP)]
    values = [pairs[d // 2][d % 2, 2 * p + 1] for p in range(PPR) for d in range(TP)]
    result = attend(shares[target, 0:16, :], keys, values, new_keys, new_values, length, me)
    rows[...] = result.astype(BF)
    last = pltpu.make_async_copy(rows, out.at[target, pl.ds(0, 16), :], row_sem.at[0])
    last.start()
    for j, slab in enumerate(slabs):
        pl.when(inst != j)(slab.wait)
    last.wait()


def turn(move_src, move_dst, lengths, shares, pairs):
    return pl.pallas_call(
        turn_kernel,
        out_shape=jax.ShapeDtypeStruct(shares.shape, BF),
        in_specs=[SMEM] * 3 + [VMEM] * (1 + TP // 2),
        out_specs=HBM,
        scratch_shapes=[
            pltpu.VMEM((16, 128), BF),
            pltpu.SemaphoreType.DMA((N_INST,)),
            pltpu.SemaphoreType.DMA((1,)),
        ],
        compiler_params=params(),
        cost_estimate=cost(3),
    )(move_src, move_dst, lengths, shares, *pairs)


def split_leaving_kernel(move_src, table, pool, own, other, sems):
    me = lax.axis_index("tp")
    leave = move_src[lax.axis_index("inst")] & (SLOTS - 1)
    copies = []
    for page in range(PPR):
        first = 2 * table[page, leave]
        for e in range(TP // 2):
            for b, ref in enumerate((own, other)):
                at = pl.multiple_of((me ^ (2 * e + b)) * 128, 128)
                copies.append(
                    pltpu.make_async_copy(
                        pool.at[pl.ds(first, 2), :, pl.ds(at, 128)],
                        ref.at[e, pl.ds(2 * page, 2)],
                        sems.at[page * TP + 2 * e + b],
                    )
                )
    for copy in copies:
        copy.start()
    for copy in copies:
        copy.wait()


def split_leaving(move_src, table, pool):
    part = jax.ShapeDtypeStruct((TP // 2, 2 * PPR, TOK, 128), BF)
    return pl.pallas_call(
        split_leaving_kernel,
        out_shape=(part, part),
        in_specs=[SMEM, SMEM, ANY],
        out_specs=(VMEM, VMEM),
        scratch_shapes=[pltpu.SemaphoreType.DMA((PPR * TP,))],
        compiler_params=params(),
        cost_estimate=cost(2),
    )(move_src, table, pool)


def split_heads_kernel(pool, own, other, sems):
    me = lax.axis_index("tp")
    copies = []
    for e in range(TP // 2):
        for b, ref in enumerate((own, other)):
            at = pl.multiple_of((me ^ (2 * e + b)) * 128, 128)
            copies.append(
                pltpu.make_async_copy(pool.at[:, :, pl.ds(at, 128)], ref.at[e], sems.at[2 * e + b])
            )
    for copy in copies:
        copy.start()
    for copy in copies:
        copy.wait()


def split_heads(pool):
    part = jax.ShapeDtypeStruct((TP // 2,) + pool.shape[:2] + (128,), BF)
    return pl.pallas_call(
        split_heads_kernel,
        out_shape=(part, part),
        in_specs=[ANY],
        out_specs=(ANY, ANY),
        scratch_shapes=[pltpu.SemaphoreType.DMA((TP,))],
        compiler_params=params(),
        cost_estimate=cost(2),
    )(pool)


def pair_kernel(own, other, *refs):
    outs, sems = refs[: TP // 2], refs[TP // 2]
    copies = []
    for e in range(TP // 2):
        for b, ref in enumerate((own, other)):
            copies.append(pltpu.make_async_copy(ref.at[e], outs[e].at[b], sems.at[2 * e + b]))
    for copy in copies:
        copy.start()
    for copy in copies:
        copy.wait()


def pair_up(own, other):
    swapped = lax.ppermute(other, "tp", [(i, i ^ 1) for i in range(TP)])
    pair = jax.ShapeDtypeStruct((2,) + own.shape[1:], BF)
    pairs = pl.pallas_call(
        pair_kernel,
        out_shape=(pair,) * (TP // 2),
        in_specs=[ANY, ANY],
        out_specs=(ANY,) * (TP // 2),
        scratch_shapes=[pltpu.SemaphoreType.DMA((TP,))],
        compiler_params=params(),
        cost_estimate=cost(1),
    )(own, swapped)
    return list(pairs)


def along_y(pairs):
    return [pairs[0]] + [
        lax.ppermute(pairs[e], "tp", [(i, i ^ (2 * e)) for i in range(TP)]) for e in range(1, TP // 2)
    ]


def silu(value):
    return value * (1.0 / (1.0 + jnp.exp(-value)))


def convolve(tail, fresh, conv_w):
    window = [tail[k : k + 1] for k in range(3)] + [fresh[k : k + 1] for k in range(2)]
    steps = []
    for t in range(2):
        total = conv_w[0:1] * window[t]
        for k in range(1, 4):
            total = total + conv_w[k : k + 1] * window[t + k]
        steps.append(total)
    return silu(jnp.concatenate(steps, 0))


def per_channel(dt_raw, a_log, dt_bias, skip):
    raw = dt_raw + dt_bias
    step = jnp.maximum(raw, 0.0) + jnp.log1p(jnp.exp(-jnp.abs(raw)))
    retain = jnp.exp(-step * jnp.exp(a_log))
    per_head = jnp.concatenate([step, retain, skip, jnp.zeros((3, HEADS), F32)], 0)
    head_row = lax.broadcasted_iota(jnp.int32, (HEADS, INNER), 0)
    channel = lax.broadcasted_iota(jnp.int32, (HEADS, INNER), 1)
    spread = jnp.where(channel // HEAD_P == head_row, 1.0, 0.0).astype(BF)
    rows = sum(dot_nn(part, spread) for part in thirds(per_head))
    return [rows[k : k + 1] for k in range(5)]


def mixer(state_dots, conv, scales, gate, gain):
    b_in = conv[:, INNER : INNER + STATE_N]
    c_out = conv[:, INNER + STATE_N :]
    step1, step2, keep1, keep2, skip_c = scales
    c_high, c_low = halves(c_out)
    dots = state_dots(jnp.concatenate([c_high, c_low, jnp.zeros((12, STATE_N), BF)], 0))
    dots = dots[0:2] + dots[2:4]
    b1, b2, c1, c2 = b_in[0:1], b_in[1:2], c_out[0:1], c_out[1:2]
    x1, x2 = conv[0:1, :INNER], conv[1:2, :INNER]
    u1, u2 = step1 * x1, step2 * x2
    bc11 = jnp.sum(b1 * c1, -1, keepdims=True)
    bc12 = jnp.sum(b1 * c2, -1, keepdims=True)
    bc22 = jnp.sum(b2 * c2, -1, keepdims=True)
    y1 = keep1 * dots[0:1] + u1 * bc11 + skip_c * x1
    y2 = keep2 * (keep1 * dots[1:2] + u1 * bc12) + u2 * bc22 + skip_c * x2
    y = jnp.concatenate([y1, y2], 0) * gate
    y = y * lax.rsqrt(jnp.mean(y * y, -1, keepdims=True) + 1e-05) * gain
    return y.astype(BF)


def mixer_all_kernel(
    move_src, state, tail, fresh, gate, dt_raw, a_log, dt_bias, skip, conv_w, gain, out, kept
):
    here = pl.program_id(0)
    slot = lax.broadcasted_iota(jnp.int32, (3, SLOTS, CONV), 1)
    mine = jnp.sum(jnp.where(slot == here, tail[...].astype(F32), 0.0), 1)
    rows = state[0].reshape(INNER, STATE_N)
    new = fresh[0].astype(F32)
    scales = per_channel(dt_raw[0], a_log[...], dt_bias[...], skip[...])
    gated = silu(gate[0].astype(F32))
    out[0] = mixer(
        lambda lhs: dot_nt(lhs, rows), convolve(mine, new, conv_w[...]), scales, gated, gain[...]
    )

    @pl.when(here == (move_src[lax.axis_index("inst")] & (SLOTS - 1)))
    def _():
        kept[0:2, :] = new
        kept[2:6, :] = conv_w[...]
        for k in range(5):
            kept[6 + k : 7 + k, 0:INNER] = scales[k]
        kept[11:13, 0:INNER] = gated
        kept[13:14, 0:INNER] = gain[...]


def mixer_all(move_src, state, tail, fresh, gate, dt_raw, a_log, dt_bias, skip, conv_w, gain):
    def whole(shape):
        return pl.BlockSpec(shape, lambda s: (0,) * len(shape))

    def by_slot(shape):
        return pl.BlockSpec((1,) + shape, lambda s: (s,) + (0,) * len(shape))

    return pl.pallas_call(
        mixer_all_kernel,
        grid=(SLOTS,),
        out_shape=(
            jax.ShapeDtypeStruct((SLOTS, 2, INNER), BF),
            jax.ShapeDtypeStruct((16, CONV), F32),
        ),
        in_specs=[
            SMEM,
            by_slot((HEADS, HEAD_P, STATE_N)),
            whole((3, SLOTS, CONV)),
            by_slot((2, CONV)),
            by_slot((2, INNER)),
            by_slot((2, HEADS)),
            whole((1, HEADS)),
            whole((1, HEADS)),
            whole((1, HEADS)),
            whole((4, CONV)),
            whole((1, INNER)),
        ],
        out_specs=(by_slot((2, INNER)), whole((16, CONV))),
        compiler_params=params(),
        cost_estimate=cost(8),
    )(move_src, state, tail, fresh, gate, dt_raw, a_log, dt_bias, skip, conv_w, gain)


def landed_kernel(
    move_src,
    move_dst,
    shares,
    kept_h,
    mixed,
    attended,
    out,
    attn_out,
    final,
    arrived,
    src_s,
    dst_s,
    final_v,
    pages,
    mixed_row,
    attn_row,
    kept,
    rows_v,
    sems,
):
    scalars = [
        pltpu.make_async_copy(move_src, src_s, sems.at[7]),
        pltpu.make_async_copy(move_dst, dst_s, sems.at[8]),
        pltpu.make_async_copy(kept_h, kept, sems.at[9]),
    ]
    for copy in scalars:
        copy.start()
    for copy in scalars[:2]:
        copy.wait()
    inst = lax.axis_index("inst")
    land = src_s[inst] & (SLOTS - 1)
    origin = sender_to(dst_s, inst)
    source = sender_to(dst_s, origin)
    for share in reversed(range(SHARES)):
        rows_v[share * ROWS : share * ROWS + ROWS, :] = shares[holder(share, origin, source)]
    for kv in range(2 * PPR):
        for head in range(TP):
            at = PAGE_AT + TOK * (kv * TP + head)
            pages[kv // 2, kv % 2, :, head * 128 : head * 128 + 128] = rows_v[at : at + TOK, :]
    sent = [pltpu.make_async_copy(pages, arrived, sems.at[0])]
    sent[0].start()
    pieces = rows_v[TAIL_AT : TAIL_AT + 64, :].astype(F32)
    tail = jnp.concatenate(
        [
            jnp.concatenate([pieces[row : row + 1] for row in range(tap * 20, tap * 20 + 20)], 1)
            for tap in range(3)
        ],
        0,
    )
    state = rows_v[0:PAGE_AT, :].reshape(HEADS, 128, 128)
    left = state[:, 0:64, :].reshape(INNER, 128)
    right = state[:, 64:128, :].reshape(INNER, 128)
    scalars[2].wait()
    conv = convolve(tail, kept[0:2, :], kept[2:6, :])
    scales = [kept[6 + k : 7 + k, 0:INNER] for k in range(5)]
    step1, step2, keep1, keep2, _ = scales
    a1 = keep2 * step1 * conv[0:1, :INNER]
    a2 = step2 * conv[1:2, :INNER]
    b1 = conv[0:1, INNER : INNER + STATE_N]
    b2 = conv[1:2, INNER : INNER + STATE_N]
    keep = keep1 * keep2
    zeros = jnp.zeros((7, INNER), F32)

    def again(value):
        high = value.astype(BF).astype(F32)
        rest = value - high
        middle = rest.astype(BF).astype(F32)
        return high, middle, rest - middle

    kh, km, kl = again(keep)
    a1h, a1l, _ = again(a1)
    a2h, a2l, _ = again(a2)
    rows = jnp.concatenate([kh, km, kl, a1h, a1l, a1h, a2h, a2l, a2h, zeros], 0)
    columns = rows.T.astype(BF)
    b1h, b1l, _ = again(b1)
    b2h, b2l, _ = again(b2)
    none = jnp.zeros((3, STATE_N), F32)
    inner = jnp.concatenate(
        [none, b1h, b1h, b1l, b2h, b2h, b2l, jnp.zeros((7, STATE_N), F32)], 0
    ).astype(BF)
    row = lax.broadcasted_iota(jnp.int32, (16, 128), 0)
    ones = jnp.where(row < 3, 1.0, 0.0).astype(BF)
    heads = 8
    block = heads * HEAD_P
    for part in range(HEADS // heads):
        at = part * block
        some = columns[at : at + block]
        share = dot_nn(some, ones)
        for half, source in enumerate((left, right)):
            added = dot_nn(some, inner[:, half * 128 : half * 128 + 128])
            result = source[at : at + block].astype(F32) * share + added
            final_v[part * heads : part * heads + heads, :, half * 128 : half * 128 + 128] = result.astype(
                BF
            ).reshape(heads, HEAD_P, 128)
        copy = pltpu.make_async_copy(
            final_v.at[pl.ds(part * heads, heads)],
            final.at[0, pl.ds(part * heads, heads)],
            sems.at[1 + part],
        )
        copy.start()
        sent.append(copy)
    rows = shares[origin, 0:16, :].astype(F32)
    attn_row[...] = jnp.concatenate([rows[2 * h : 2 * h + 2] for h in range(8)], 1).astype(BF)
    sent.append(pltpu.make_async_copy(attn_row, attn_out.at[land], sems.at[5]))
    sent[-1].start()
    mixed_row[...] = mixer(
        lambda lhs: dot_nt(lhs[:, :128], left) + dot_nt(lhs[:, 128:], right),
        conv,
        scales,
        kept[11:13, 0:INNER],
        kept[13:14, 0:INNER],
    )
    sent.append(pltpu.make_async_copy(mixed_row, out.at[land], sems.at[6]))
    sent[-1].start()
    for copy in sent:
        copy.wait()


def landed(move_src, move_dst, shares, kept, mixed, attended):
    return pl.pallas_call(
        landed_kernel,
        out_shape=(
            jax.ShapeDtypeStruct(mixed.shape, BF),
            jax.ShapeDtypeStruct(attended.shape, BF),
            jax.ShapeDtypeStruct((1, HEADS, HEAD_P, STATE_N), BF),
            jax.ShapeDtypeStruct((PPR, 2, TOK, TP * 128), BF),
        ),
        in_specs=[ANY, ANY, VMEM, ANY, ANY, ANY],
        out_specs=(ANY,) * 4,
        input_output_aliases={4: 0, 5: 1},
        scratch_shapes=[
            pltpu.SMEM(move_src.shape, jnp.int32),
            pltpu.SMEM(move_dst.shape, jnp.int32),
            pltpu.VMEM((HEADS, HEAD_P, STATE_N), BF),
            pltpu.VMEM((PPR, 2, TOK, TP * 128), BF),
            pltpu.VMEM(mixed.shape[1:], BF),
            pltpu.VMEM(attended.shape[1:], BF),
            pltpu.VMEM(kept.shape, F32),
            pltpu.VMEM((ALL_ROWS, 128), BF),
            pltpu.SemaphoreType.DMA((10,)),
        ],
        compiler_params=params(),
        cost_estimate=cost(4),
    )(in_hbm(move_src), in_hbm(move_dst), shares, in_hbm(kept), in_hbm(mixed), in_hbm(attended))


def attend(q_rows, keys, values, new_keys, new_values, length, flip):
    pad = jnp.zeros((TOK - 2, 128), F32)
    new_keys = jnp.concatenate([new_keys, pad], 0).astype(BF)
    new_values = jnp.concatenate([new_values, pad], 0).astype(BF)
    cached = PPR * TP * TOK
    all_keys = jnp.concatenate(keys + [new_keys], 0)
    all_values = jnp.concatenate(values + [new_values], 0)
    scores = dot_nt(q_rows, all_keys) * (HEAD_D**-0.5)
    shape = (16, cached + TOK)
    column = lax.broadcasted_iota(jnp.int32, shape, 1)
    step = lax.broadcasted_iota(jnp.int32, shape, 0) & 1
    held = (column >> 4) & (TP - 1)
    position = (column & ~127) + ((held ^ flip) << 4) + (column & 15)
    allowed = jnp.where(column < cached, position - length, column - cached - step - 1) < 0
    peak = jnp.max(jnp.where(allowed, scores, -1e30), -1, keepdims=True)
    weights = jnp.where(allowed, jnp.exp(scores - peak), 0.0)
    total = jnp.sum(weights, -1, keepdims=True)
    high, low = halves(weights)
    return (dot_nn(high, all_values) + dot_nn(low, all_values)) / total


def attend_all_kernel(table, lengths, queries, new_kv, *refs):
    pairs, out = refs[: TP // 2], refs[TP // 2]
    inst, me = lax.axis_index("inst"), lax.axis_index("tp")

    def one(slot, carry):
        keys, values = [], []
        for page in range(PPR):
            at = table[page, slot]
            for d in range(TP):
                keys.append(pairs[d // 2][d % 2, 2 * at])
                values.append(pairs[d // 2][d % 2, 2 * at + 1])
        length = lengths[inst * SLOTS + slot]
        q_rows = head_rows(queries[slot].astype(F32)).astype(BF)
        fresh = new_kv[slot].astype(F32)
        rows = attend(q_rows, keys, values, fresh[:, 0], fresh[:, 1], length, me)
        out[slot] = jnp.concatenate([rows[2 * h : 2 * h + 2] for h in range(8)], 1).astype(BF)
        return carry

    lax.fori_loop(0, SLOTS, one, 0)


def attend_all(table, lengths, queries, new_kv, pairs):
    return pl.pallas_call(
        attend_all_kernel,
        out_shape=jax.ShapeDtypeStruct(queries.shape, BF),
        in_specs=[SMEM, SMEM] + [VMEM] * (2 + TP // 2),
        out_specs=VMEM,
        compiler_params=params(),
        cost_estimate=cost(4),
    )(table, lengths, queries, new_kv, *pairs)


def shards(
    ssm_state,
    conv_tail,
    kv_pool,
    page_table,
    lengths,
    move_src,
    move_dst,
    x_in,
    z_gate,
    dt_raw,
    queries,
    new_kv,
    a_log,
    dt_bias,
    skip_d,
    conv_w,
    norm_gain,
):
    tail = jnp.transpose(conv_tail, (1, 0, 2))
    table = jnp.transpose(page_table, (1, 0))
    a_row, bias_row, skip_row = a_log[None], dt_bias[None], skip_d[None]
    gain_row = norm_gain[None]
    small = (x_in, z_gate, dt_raw, a_row, bias_row, skip_row, conv_w, gain_row)

    packed = pack(move_src, move_dst, table, ssm_state, tail, kv_pool, queries, new_kv)
    spread = lax.all_to_all(packed, "inst", 0, 0, tiled=True)

    pool = kv_pool.reshape((-1,) + kv_pool.shape[2:])
    leaving = along_y(pair_up(*split_leaving(move_src, table, pool)))
    pairs = pair_up(*split_heads(pool))
    mixed, kept = mixer_all(move_src, ssm_state, tail, *small)
    spread, mixed, kept, pairs, leaving = lax.optimization_barrier(
        (spread, mixed, kept, pairs, leaving)
    )

    turned = turn(move_src, move_dst, lengths, spread, leaving)
    turned, pairs = lax.optimization_barrier((turned, pairs))
    shares = lax.all_to_all(turned, "inst", 0, 0, tiled=True)

    attended = attend_all(table, lengths, queries, new_kv, along_y(pairs))
    mamba_out, attn_out, arrived_state, arrived_pages = landed(
        move_src, move_dst, shares, kept, mixed, attended
    )
    return mamba_out, attn_out, arrived_state, arrived_pages


def solution(mesh):
    in_specs = (
        P("inst", "tp", None, None),
        P("inst", None, "tp"),
        P("inst", None, "tp", None),
        P("inst", None),
        P(),
        P(),
        P(),
        P("inst", None, "tp"),
        P("inst", None, "tp"),
        P("inst", None, "tp"),
        P("inst", None, "tp"),
        P("inst", None, None, "tp"),
        P("tp"),
        P("tp"),
        P("tp"),
        P(None, "tp"),
        P("tp"),
    )
    out_specs = (
        P("inst", None, "tp"),
        P("inst", None, "tp"),
        P("inst", "tp", None, None),
        P("inst", None, "tp", None),
    )
    return jax.shard_map(shards, mesh=mesh, in_specs=in_specs, out_specs=out_specs, check_vma=False)
```
